256 devices in a mesh: col: 16 (over y, x), height: 16 (over z, core).
Axes of the slice: x: 4, y: 4, z: 8, core: 2. Of those that a mesh axis runs over, the one named last changes fastest.
Arguments:
- orbitals: bfloat16 [192, 128, 256, 128], P('col', 'height'), may hold values from -6 to 6
- live_atoms: int32 [192, 128], P('col', 'height'), may hold values from 1 to 4
- pair_index: int32 [192, 128, 4, 4], P('col', 'height'), may hold values from 0 to 255
- density_blocks: bfloat16 [4096, 64, 64], P(('col', 'height')), may hold values from -0.0234375 to 0.0234375
Outputs:
- potential: float32 [192, 128, 128], P('col', 'height')
- hamiltonian: float32 [4096, 64, 64], P(('col', 'height'))
The draws below stay inside these ranges and needn't reach their ends.
Inputs may be any that keep to these rules, and one draw needn't show every extreme that they name: A line's live atom blocks are its first live_atoms blocks. `pair_index`: indices are local to the column group: line x uses blocks x // 12 * 256 onward.
All inputs are finite; a program needn't handle non-finite values.
Results may differ from the reference program's by a relative error of at most 0.006.
Values may be sent and summed in bfloat16 or wider, within the bound.
No kernel may reach another device: no remote copies, remote signals or barrier semaphores. Data moves between devices by JAX's collectives and lax.ppermute only.
A program may use at most 128 MiB of HBM per device.

```python
import jax
import jax.numpy as jnp
from jax import lax

ORB = 64
NA = 4
NY = 128
CX = 12
NX = 192
NZ = 128
DB_COL = 256
DB_TOTAL = 4096
N_COL = 16


def set_ends(array, own_key, least, top_value):
    longest = array.shape.index(max(array.shape))
    spots = []
    for shift in (0, 1):
        where = [jax.random.randint(jax.random.fold_in(own_key, axis), (), 0, length) for axis, length in enumerate(array.shape)]
        where[longest] = (where[longest] + shift) % array.shape[longest]
        spots.append(tuple(where))
    return array.at[spots[0]].set(least).at[spots[1]].set(top_value)


def level_of(key, dims, shards, smallest, high):
    factor_of = 1.0
    for axis_at, shards_of in shards:
        heights = jax.random.uniform(jax.random.fold_in(jax.random.fold_in(key, 6), axis_at), (shards_of,), jnp.float32, smallest / len(shards), high / len(shards))
        factor_of = factor_of * jnp.repeat(jnp.exp(heights), dims[axis_at] // shards_of).reshape((-1,) + (1,) * (len(dims) - 1 - axis_at))
    return factor_of


def centred(rng, dims, scale, bound, cuts=(), held_as=jnp.bfloat16):
    result = scale * jax.random.normal(rng, dims, jnp.float32)
    if cuts:
        result = result * level_of(rng, dims, cuts, -0.22, 0.18)
    return jnp.clip(result, -bound, bound).astype(held_as)


def setup_inputs(seed: int = 0) -> dict:
    key_list = jax.random.split(jax.random.key(seed), 5)
    orbitals = centred(key_list[0], (NX, NZ, NA * ORB, NY), 1.0, 6.0, ((0, 16), (1, 16)))
    live_atoms = set_ends(jax.random.randint(key_list[1], (NX, NZ), 1, NA + 1), jax.random.fold_in(key_list[1], 1), 1, NA).astype(jnp.int32)
    pair_index = set_ends(jax.random.randint(key_list[2], (NX, NZ, NA, NA), 0, DB_COL), jax.random.fold_in(key_list[2], 1), 0, DB_COL - 1).astype(jnp.int32)
    density_blocks = centred(key_list[3], (DB_TOTAL, ORB, ORB), (1.0 / (NA * ORB)), 0.0234375, ((0, 256),))
    return dict(orbitals=orbitals, live_atoms=live_atoms, pair_index=pair_index, density_blocks=density_blocks)


XC_COEF = 0.7386
FOUR_PI = 12.566370614359172
KAPPA = 0.5


def symbol(count):
    steps = jnp.arange(count, dtype=jnp.float32)
    return 2.0 - 2.0 * jnp.cos(2.0 * jnp.pi * steps / count)


def reference(orbitals, live_atoms, pair_index, density_blocks):
    orbital_width = NA * ORB
    atom_of = jnp.arange(orbital_width, dtype=jnp.int32) // ORB
    live_mask = (atom_of[None, None, :] < live_atoms[:, :, None]).astype(jnp.bfloat16)
    masked = orbitals * live_mask[..., None]
    start_positions = (jnp.arange(NX, dtype=jnp.int32) // CX) * DB_COL

    def tile_density(orbital_row_values, pair_row_values, base):
        chosen = density_blocks[base + pair_row_values]
        block_matrix = chosen.transpose(0, 2, 1, 3).reshape(orbital_width, orbital_width)
        product = jnp.dot(block_matrix, orbital_row_values, preferred_element_type=jnp.float32)
        return jnp.sum(orbital_row_values.astype(jnp.float32) * product, axis=0)

    def plane_density(operands):
        orbital_plane, pair_plane, base = operands
        return jax.vmap(lambda rows_one, pairs_one: tile_density(rows_one, pairs_one, base))(orbital_plane, pair_plane)

    density = lax.map(plane_density, (masked, pair_index, start_positions))
    symbol_sum = symbol(NX)[:, None, None] + symbol(NZ)[None, :, None] + symbol(NY)[None, None, :]
    kernel = FOUR_PI / (symbol_sum + KAPPA * KAPPA)
    hartree = jnp.real(jnp.fft.ifftn(jnp.fft.fftn(density) * kernel))
    potential = hartree - XC_COEF * jnp.power(density * density + 1.0, 1.0 / 6.0)

    def column_blocks(operands):
        orbital_group, pair_group, potential_group = operands

        def line_terms(summed, line_ops):
            orbital_plane, pair_plane, potential_plane = line_ops
            weight_applied = (orbital_plane.astype(jnp.float32) * potential_plane[:, None, :]).astype(jnp.bfloat16)
            full_block = jnp.einsum('zap,zbp->zab', weight_applied.astype(jnp.float32), orbital_plane.astype(jnp.float32))
            pieces = full_block.reshape(NZ, NA, ORB, NA, ORB).transpose(0, 1, 3, 2, 4).reshape(NZ * NA * NA, ORB * ORB)
            added = jax.ops.segment_sum(pieces, pair_plane.reshape(-1).astype(jnp.int32), num_segments=DB_COL)
            return summed + added, None

        start = jnp.zeros((DB_COL, ORB * ORB), jnp.float32)
        summed, _ = lax.scan(line_terms, start, (orbital_group, pair_group, potential_group))
        return summed

    grouped = (masked.reshape(N_COL, CX, NZ, orbital_width, NY), pair_index.reshape(N_COL, CX, NZ, NA, NA), potential.reshape(N_COL, CX, NZ, NY))
    hamiltonian = lax.map(column_blocks, grouped).reshape(DB_TOTAL, ORB, ORB)
    return potential, hamiltonian
```

```python
import math

import jax
import jax.numpy as jnp
import numpy as np
from jax import lax
from jax.experimental import pallas as pl
from jax.experimental.pallas import tpu as pltpu
from jax.sharding import PartitionSpec as P

XC_COEF = 0.7386
FOUR_PI = 12.566370614359172
KAPPA = 0.5
LANES = 128
F32 = jnp.float32
BF16 = jnp.bfloat16
HIGHEST = lax.Precision.HIGHEST
VMEM_LIMIT = 56 * 1024 * 1024


def cas_table(count):
    steps = np.arange(count)
    angle = 2.0 * np.pi * (steps[:, None] * steps[None, :] % count) / count
    return (np.cos(angle) + np.sin(angle)).astype(np.float32)


def symbol(count):
    return (2.0 - 2.0 * np.cos(2.0 * np.pi * np.arange(count) / count)).astype(np.float32)


def density_kernel(pair_ref, live_ref, base_ref, orb_ref, *refs):
    pieces, (cas_ref, dens_ref, spec_ref, table_ref) = refs[:-4], refs[-4:]
    step = pl.program_id(0)
    group = orb_ref.shape[0]
    packed_rows = table_ref.shape[0] // 2

    @pl.when(step == 0)
    def _():
        at = 0
        for piece in pieces:
            for first in range(0, piece.shape[0], 8):
                base = base_ref[at]
                at += 1
                both = piece[first : first + 8]
                table_ref[pl.ds(base, 8)] = both
                table_ref[pl.ds(packed_rows + base, 8)] = jnp.concatenate(
                    [both[:, :, 64:], both[:, :, :64]], axis=2
                )

    left_lanes = lax.broadcasted_iota(jnp.int32, (64, LANES), 1) < 64

    def place(p, side):
        row = (p >> 4) * 8 + (p & 7)
        other = (p >> 3) & 1
        return row + (other if side == 0 else 1 - other) * packed_rows

    rows_out = []
    for l in range(group):
        line = step * group + l
        live = live_ref[line]
        phi = jnp.concatenate(
            [
                jnp.where(a < live, orb_ref[l, a * 64 : (a + 1) * 64, :], jnp.zeros((), BF16))
                for a in range(4)
            ],
            axis=0,
        )
        strips = []
        for a in range(4):
            halves = []
            for b in (0, 2):
                p0 = pair_ref[line * 16 + a * 4 + b]
                p1 = pair_ref[line * 16 + a * 4 + b + 1]
                halves.append(jnp.where(left_lanes, table_ref[place(p0, 0)], table_ref[place(p1, 1)]))
            strips.append(jnp.concatenate(halves, axis=1))
        matrix = jnp.concatenate(strips, axis=0)
        product = jnp.dot(matrix, phi, preferred_element_type=F32)
        rows_out.append(jnp.sum(phi.astype(F32) * product, axis=0, keepdims=True))
    dens_ref[pl.ds(pl.multiple_of(step * group, group), group), :] = jnp.concatenate(rows_out, axis=0)

    @pl.when(step == pl.num_programs(0) - 1)
    def _():
        spectrum = jnp.dot(dens_ref[...], cas_ref[...], precision=HIGHEST, preferred_element_type=F32)
        lines = spectrum.shape[0]
        wide = jnp.concatenate([spectrum, jnp.zeros((LANES - lines, spectrum.shape[1]), F32)], axis=0)
        spec_ref[...] = wide.T


def solve_kernel(part_ref, in_ref, cx_ref, cxt_ref, cz_ref, sx_ref, sz_ref, sy_ref, out_ref, *, cells_x, cells_z, cols, heights):
    core = part_ref[0]
    plane = part_ref[1]
    lane = lax.broadcasted_iota(jnp.int32, (cols, LANES), 1)
    group_of = lane // cells_z
    slots = LANES // cells_z
    skewed = [
        pltpu.roll(in_ref[pl.ds(h, cols, stride=heights), :], cells_z * h, 1) if h else in_ref[pl.ds(h, cols, stride=heights), :]
        for h in range(heights)
    ]
    rows = []
    for x in range(cells_x):
        mixed = jnp.zeros((cols, LANES), F32)
        for g in range(slots):
            mixed = jnp.where(group_of == g, skewed[(g - x) % slots], mixed)
        rows.append(pltpu.roll(mixed, LANES - cells_z * x, 1) if x else mixed)
    field = jnp.concatenate(rows, axis=0)
    forward = cx_ref[core]
    spec = jnp.dot(forward, field, precision=HIGHEST, preferred_element_type=F32)
    spec = jnp.dot(spec, cz_ref[...], precision=HIGHEST, preferred_element_type=F32)
    scale = sx_ref[core] + sz_ref[...] + sy_ref[plane]
    spec = spec / scale
    spec = jnp.dot(spec, cz_ref[...], precision=HIGHEST, preferred_element_type=F32)
    back = jnp.dot(cxt_ref[core], spec, precision=HIGHEST, preferred_element_type=F32)
    skewed = []
    for x in range(cells_x):
        part = back[x * cols : (x + 1) * cols]
        skewed.append(pltpu.roll(part, cells_z * x, 1) if x else part)
    for h in range(heights):
        mixed = jnp.zeros((cols, LANES), F32)
        for x in range(cells_x):
            mixed = jnp.where(group_of == (h + x) % slots, skewed[x], mixed)
        mixed = pltpu.roll(mixed, LANES - cells_z * h, 1) if h else mixed
        out_ref[pl.ds(h, cols, stride=heights), :] = mixed


def hamiltonian_kernel(
    pair_ref, live_ref, base_ref, orb_ref, dens_ref, back_ref, cas_ref, pot_ref, keep_ref, first_ref, rest_ref, acc_ref
):
    step = pl.program_id(0)
    group = orb_ref.shape[0]
    lines = dens_ref.shape[0]

    @pl.when(step == 0)
    def _():
        hartree = lax.dot_general(
            back_ref[...].T, cas_ref[...], (((1,), (0,)), ((), ())), precision=HIGHEST, preferred_element_type=F32
        )
        dens = dens_ref[...]
        pot_ref[...] = hartree[:lines] - XC_COEF * jnp.exp(jnp.log(dens * dens + 1.0) * (1.0 / 6.0))

        def clear(i, carry):
            acc_ref[pl.ds(i * 8, 8)] = jnp.zeros((8, 64, LANES), F32)
            return carry

        lax.fori_loop(0, acc_ref.shape[0] // 8, clear, 0)

    potential = pot_ref[pl.ds(pl.multiple_of(step * group, group), group), :]
    for l in range(group):
        line = step * group + l
        live = live_ref[line]
        phi = jnp.concatenate(
            [
                jnp.where(a < live, orb_ref[l, a * 64 : (a + 1) * 64, :], jnp.zeros((), BF16))
                for a in range(4)
            ],
            axis=0,
        )
        weighted = (phi.astype(F32) * potential[l : l + 1, :]).astype(BF16)
        full = lax.dot_general(weighted, phi, (((1,), (1,)), ((), ())), preferred_element_type=F32)
        for a in range(4):
            for b in (0, 2):
                p0 = pair_ref[line * 16 + a * 4 + b]
                p1 = pair_ref[line * 16 + a * 4 + b + 1]
                both = full[a * 64 : (a + 1) * 64, b * 64 : b * 64 + LANES]
                acc_ref[p0] += both
                acc_ref[p1] += pltpu.roll(both, 64, 1)

    @pl.when(step == pl.num_programs(0) - 1)
    def _():
        left_lanes = lax.broadcasted_iota(jnp.int32, (8, 64, LANES), 2) < 64
        at = 0
        for out in (keep_ref, first_ref, rest_ref):
            for first in range(0, out.shape[0], 8):
                base = base_ref[at]
                at += 1
                low = acc_ref[pl.ds(base, 8)]
                high = acc_ref[pl.ds(base + 8, 8)]
                out[first : first + 8] = jnp.where(left_lanes, low, pltpu.roll(high, 64, 2)).astype(out.dtype)


def per_device(orbitals, live_atoms, pair_index, density_blocks):
    cells_x, cells_z, width, line_cells = orbitals.shape
    cols = lax.axis_size("col")
    heights = lax.axis_size("height")
    full_x = cells_x * cols
    full_z = cells_z * heights
    lines = cells_x * cells_z
    share = density_blocks.shape[0]
    devices = cols * heights
    copies = devices // line_cells
    group = 8
    block_rows = share * heights // 2

    cas_y = cas_table(line_cells)
    cas_y2 = np.repeat(cas_y, copies, axis=1)
    cas_x = cas_table(full_x)
    order = np.arange(full_x).reshape(cols, cells_x).T.reshape(-1)
    half_x = full_x // copies
    forward_x = cas_x.reshape(copies, half_x, full_x)[:, :, order]
    back_x = forward_x.transpose(0, 2, 1).copy()
    cas_z = cas_table(full_z)
    norm = 1.0 / (full_x * full_z * line_cells)
    unit = FOUR_PI * norm
    sym_x = np.broadcast_to(symbol(full_x).reshape(copies, half_x, 1) / unit, (copies, half_x, LANES)).astype(np.float32)
    sym_z = ((symbol(full_z) + KAPPA * KAPPA) / unit).reshape(1, full_z).astype(np.float32)
    sym_y = (symbol(line_cells) / unit).astype(np.float32)

    orb = orbitals.reshape(lines, width, line_cells)
    live = live_atoms.reshape(lines)
    pairs = pair_index.reshape(lines * 16)
    packed = jnp.concatenate([density_blocks[: share // 2], density_blocks[share // 2 :]], axis=2)
    chips = heights // 2
    far = chips // 2
    height = lax.axis_index("height")
    chip, core = height // 2, height % 2
    turn = 1 - 2 * core
    twin = [(h, h ^ 1) for h in range(heights)]
    ring = [(h, (h + 2 - 4 * (h % 2)) % heights) for h in range(heights)]

    def across(values):
        return lax.ppermute(values, "height", twin)

    def onward(values):
        return lax.ppermute(values, "height", ring)

    def place_of(distance, owner):
        return ((chip + distance) % chips) * 2 + owner

    moving = jnp.concatenate([packed, across(packed)], axis=0)
    pieces = [moving]
    heights_of = [place_of(0, core), place_of(0, 1 - core)]
    for d in range(1, far + 1):
        moving = onward(moving if d < far else moving[: share // 2])
        pieces += [moving, across(moving)]
        if d < far:
            heights_of += [place_of(-turn * d, core), place_of(-turn * d, 1 - core)]
            heights_of += [place_of(turn * d, 1 - core), place_of(turn * d, core)]
        else:
            heights_of += [place_of(d, core), place_of(d, 1 - core)]
    table_rows = (jnp.stack(heights_of) * (share // 2)).astype(jnp.int32)
    keep_of, give_of = [], []
    for d in range(far, -1, -1):
        keep_of.append(place_of(turn * d, core))
        give_of.append(place_of(-turn * d, 1 - core))
        if 0 < d < far:
            keep_of.append(place_of(turn * d, 1 - core))
            give_of.append(place_of(-turn * d, core))
    sum_rows = (jnp.stack(keep_of + give_of) * share).astype(jnp.int32)

    def whole(*shape):
        return pl.BlockSpec(shape, lambda i, *_: (0,) * len(shape))

    params = pltpu.CompilerParams(dimension_semantics=("arbitrary",), vmem_limit_bytes=VMEM_LIMIT)
    density, spectrum = pl.pallas_call(
        density_kernel,
        grid_spec=pltpu.PrefetchScalarGridSpec(
            num_scalar_prefetch=3,
            grid=(lines // group,),
            in_specs=[
                pl.BlockSpec((group, width, line_cells), lambda i, *_: (i, 0, 0)),
                *[whole(*piece.shape) for piece in pieces],
                whole(line_cells, devices),
            ],
            out_specs=[whole(lines, line_cells), whole(devices, LANES)],
            scratch_shapes=[pltpu.VMEM((2 * block_rows, 64, LANES), BF16)],
        ),
        out_shape=[
            jax.ShapeDtypeStruct((lines, line_cells), F32),
            jax.ShapeDtypeStruct((devices, LANES), F32),
        ],
        compiler_params=params,
        name="density",
    )(pairs, live, table_rows, orb, *pieces, jnp.asarray(cas_y2))

    def exchange(values):
        out = lax.all_to_all(values.reshape(devices, 1, LANES), ("col", "height"), split_axis=0, concat_axis=0, tiled=True)
        return out.reshape(devices, LANES)

    device = lax.axis_index("col") * heights + height
    part = jnp.stack([device % copies, device // copies]).astype(jnp.int32)
    smem = pl.BlockSpec(memory_space=pltpu.SMEM)
    vmem = pl.BlockSpec(memory_space=pltpu.VMEM)
    solved = pl.pallas_call(
        lambda *refs: solve_kernel(*refs, cells_x=cells_x, cells_z=cells_z, cols=cols, heights=heights),
        in_specs=[smem, vmem, vmem, vmem, vmem, vmem, vmem, smem],
        out_specs=vmem,
        out_shape=jax.ShapeDtypeStruct((devices, LANES), F32),
        compiler_params=pltpu.CompilerParams(vmem_limit_bytes=VMEM_LIMIT),
        name="solve",
    )(
        part,
        exchange(spectrum),
        jnp.asarray(forward_x),
        jnp.asarray(back_x),
        jnp.asarray(cas_z),
        jnp.asarray(sym_x),
        jnp.asarray(sym_z),
        jnp.asarray(sym_y),
    )
    returned = exchange(solved)

    half_rows = block_rows // 2
    potential, keep, give_first, give_rest = pl.pallas_call(
        hamiltonian_kernel,
        grid_spec=pltpu.PrefetchScalarGridSpec(
            num_scalar_prefetch=3,
            grid=(lines // group,),
            in_specs=[
                pl.BlockSpec((group, width, line_cells), lambda i, *_: (i, 0, 0)),
                whole(lines, line_cells),
                whole(devices, LANES),
                whole(devices, line_cells),
            ],
            out_specs=[
                whole(lines, line_cells),
                whole(half_rows, 64, LANES),
                whole(share // 2, 64, LANES),
                whole(half_rows - share // 2, 64, LANES),
            ],
            scratch_shapes=[pltpu.VMEM((2 * block_rows, 64, LANES), F32)],
        ),
        out_shape=[
            jax.ShapeDtypeStruct((lines, line_cells), F32),
            jax.ShapeDtypeStruct((half_rows, 64, LANES), F32),
            jax.ShapeDtypeStruct((share // 2, 64, LANES), BF16),
            jax.ShapeDtypeStruct((half_rows - share // 2, 64, LANES), BF16),
        ],
        compiler_params=params,
        name="hamiltonian",
    )(pairs, live, sum_rows, orb, density, returned, jnp.asarray(cas_y2.T.copy()))

    half = share // 2
    got_first = across(give_first)
    got_rest = across(give_rest)
    moving = onward((keep[:half] + got_first.astype(F32)).astype(BF16)).astype(F32)
    for i, d in enumerate(range(far - 1, 0, -1)):
        at = half + share * i
        terms = keep[at : at + share] + got_rest[at - half : at - half + share].astype(F32)
        if i == 0:
            moving = jnp.concatenate([moving, jnp.zeros_like(moving)], axis=0)
        moving = onward((terms + moving).astype(BF16)).astype(F32)
    other = across(moving[half:].astype(BF16)).astype(F32)
    summed = keep[half_rows - half :] + got_rest[-half:].astype(F32) + moving[:half] + other
    hamiltonian = jnp.concatenate([summed[:, :, :64], summed[:, :, 64:]], axis=0)
    return potential.reshape(cells_x, cells_z, line_cells), hamiltonian


def solution(mesh):
    placed = (
        P("col", "height", None, None),
        P("col", "height"),
        P("col", "height", None, None),
        P(("col", "height"), None, None),
    )
    return jax.shard_map(
        per_device,
        mesh=mesh,
        in_specs=placed,
        out_specs=(P("col", "height", None), P(("col", "height"), None, None)),
        check_vma=False,
    )
```

```python
import functools

import jax
import jax.numpy as jnp
import numpy as np
from jax import lax
from jax.experimental import pallas as pl
from jax.experimental.pallas import tpu as pltpu
from jax.sharding import PartitionSpec as P

XC_COEF = 0.7386
FOUR_PI = 12.566370614359172
KAPPA = 0.5
LANES = 128
F32 = jnp.float32
BF16 = jnp.bfloat16
HIGHEST = lax.Precision.HIGHEST
VMEM_LIMIT = 56 * 1024 * 1024


def cas_table(count):
    steps = np.arange(count)
    angle = 2.0 * np.pi * (steps[:, None] * steps[None, :] % count) / count
    return (np.cos(angle) + np.sin(angle)).astype(np.float32)


def symbol(count):
    return (2.0 - 2.0 * np.cos(2.0 * np.pi * np.arange(count) / count)).astype(np.float32)


def masked_line(orb_ref, line, live):
    parts = []
    for a in range(4):
        rows = orb_ref[line, a * 64 : (a + 1) * 64, :]
        parts.append(rows if a == 0 else jnp.where(a < live, rows, jnp.zeros((), BF16)))
    return jnp.concatenate(parts, axis=0)


def orbital_copies(orb_hbm, orb_ref, sems, chunk):
    return [
        pltpu.make_async_copy(orb_hbm.at[pl.ds(i * chunk, chunk)], orb_ref.at[pl.ds(i * chunk, chunk)], sems.at[i])
        for i in range(orb_ref.shape[0] // chunk)
    ]


def density_kernel(index_ref, live_ref, base_ref, orb_hbm, *refs, chunk):
    pieces, (cas_ref, dens_ref, spec_ref, orb_ref, table_ref, orb_sems, table_sems) = refs[:-7], refs[-7:]
    packed_rows = table_ref.shape[0] // 2
    copies = []
    for piece in pieces:
        for first in range(0, piece.shape[0], 8):
            i = len(copies)
            rows = table_ref.at[pl.ds(base_ref[i], 8)]
            copies.append(pltpu.make_async_copy(piece.at[pl.ds(first, 8)], rows, table_sems.at[i]))
    for copy in copies:
        copy.start()
    for copy in orbital_copies(orb_hbm, orb_ref, orb_sems, chunk):
        copy.start()
    for copy in copies:
        copy.wait()

    def fill(i, carry):
        both = table_ref[pl.ds(i * 8, 8)]
        table_ref[pl.ds(packed_rows + i * 8, 8)] = pltpu.roll(both, 64, 2)
        return carry

    lax.fori_loop(0, packed_rows // 8, fill, 0)
    left_lanes = lax.broadcasted_iota(jnp.int32, (64, LANES), 1) < 64

    def body(i, carry):
        first = i * chunk
        pltpu.make_async_copy(orb_hbm.at[pl.ds(first, chunk)], orb_ref.at[pl.ds(first, chunk)], orb_sems.at[i]).wait()
        rows_out = []
        for l in range(chunk):
            line = first + l
            phi = masked_line(orb_ref, line, live_ref[line])
            strips = []
            for a in range(4):
                halves = []
                for b in (0, 2):
                    at = line * 16 + a * 4 + b
                    halves.append(jnp.where(left_lanes, table_ref[index_ref[at]], table_ref[index_ref[at + 1]]))
                strips.append(jnp.concatenate(halves, axis=1))
            matrix = jnp.concatenate(strips, axis=0)
            product = jnp.dot(matrix, phi, preferred_element_type=F32)
            rows_out.append(jnp.sum(phi.astype(F32) * product, axis=0, keepdims=True))
        dens_ref[pl.ds(pl.multiple_of(first, 8), chunk), :] = jnp.concatenate(rows_out, axis=0)
        return carry

    lax.fori_loop(0, orb_ref.shape[0] // chunk, body, 0)
    spectrum = jnp.dot(dens_ref[...], cas_ref[...], precision=HIGHEST, preferred_element_type=F32)
    lines = spectrum.shape[0]
    wide = jnp.concatenate([spectrum, jnp.zeros((LANES - lines, spectrum.shape[1]), F32)], axis=0)
    spec_ref[...] = wide.T


def solve_kernel(part_ref, in_ref, cx_ref, cxt_ref, cz_ref, sx_ref, sz_ref, sy_ref, out_ref, *, cells_x, cells_z, cols, heights):
    core = part_ref[0]
    plane = part_ref[1]
    lane = lax.broadcasted_iota(jnp.int32, (cols, LANES), 1)
    group_of = lane // cells_z
    slots = LANES // cells_z
    skewed = [
        pltpu.roll(in_ref[pl.ds(h, cols, stride=heights), :], cells_z * h, 1) if h else in_ref[pl.ds(h, cols, stride=heights), :]
        for h in range(heights)
    ]
    rows = []
    for x in range(cells_x):
        mixed = jnp.zeros((cols, LANES), F32)
        for g in range(slots):
            mixed = jnp.where(group_of == g, skewed[(g - x) % slots], mixed)
        rows.append(pltpu.roll(mixed, LANES - cells_z * x, 1) if x else mixed)
    field = jnp.concatenate(rows, axis=0)
    forward = cx_ref[core]
    spec = jnp.dot(forward, field, precision=HIGHEST, preferred_element_type=F32)
    spec = jnp.dot(spec, cz_ref[...], precision=HIGHEST, preferred_element_type=F32)
    scale = sx_ref[core] + sz_ref[...] + sy_ref[plane]
    spec = spec / scale
    spec = jnp.dot(spec, cz_ref[...], precision=HIGHEST, preferred_element_type=F32)
    back = jnp.dot(cxt_ref[core], spec, precision=HIGHEST, preferred_element_type=F32)
    skewed = []
    for x in range(cells_x):
        part = back[x * cols : (x + 1) * cols]
        skewed.append(pltpu.roll(part, cells_z * x, 1) if x else part)
    for h in range(heights):
        mixed = jnp.zeros((cols, LANES), F32)
        for x in range(cells_x):
            mixed = jnp.where(group_of == (h + x) % slots, skewed[x], mixed)
        mixed = pltpu.roll(mixed, LANES - cells_z * h, 1) if h else mixed
        out_ref[pl.ds(h, cols, stride=heights), :] = mixed


def hamiltonian_kernel(
    pair_ref,
    live_ref,
    base_ref,
    orb_hbm,
    dens_ref,
    back_ref,
    cas_ref,
    pot_ref,
    keep_hbm,
    first_hbm,
    rest_hbm,
    orb_ref,
    left_ref,
    right_ref,
    keep_ref,
    give_ref,
    orb_sems,
    out_sems,
    *,
    chunk,
):
    lines = dens_ref.shape[0]
    for copy in orbital_copies(orb_hbm, orb_ref, orb_sems, chunk):
        copy.start()

    def clear(i, carry):
        left_ref[pl.ds(i * 8, 8)] = jnp.zeros((8, 64, LANES), F32)
        right_ref[pl.ds(i * 8, 8)] = jnp.zeros((8, 64, LANES), F32)
        return carry

    lax.fori_loop(0, left_ref.shape[0] // 8, clear, 0)
    hartree = lax.dot_general(
        back_ref[...].T, cas_ref[...], (((1,), (0,)), ((), ())), precision=HIGHEST, preferred_element_type=F32
    )
    dens = dens_ref[...]
    pot_ref[...] = hartree[:lines] - XC_COEF * jnp.exp(jnp.log(dens * dens + 1.0) * (1.0 / 6.0))

    def body(i, carry):
        first = i * chunk
        pltpu.make_async_copy(orb_hbm.at[pl.ds(first, chunk)], orb_ref.at[pl.ds(first, chunk)], orb_sems.at[i]).wait()
        potential = pot_ref[pl.ds(pl.multiple_of(first, 8), chunk), :]
        for l in range(chunk):
            line = first + l
            phi = masked_line(orb_ref, line, live_ref[line])
            weighted = (phi.astype(F32) * potential[l : l + 1, :]).astype(BF16)
            full = lax.dot_general(weighted, phi, (((1,), (1,)), ((), ())), preferred_element_type=F32)
            for a in range(4):
                for b in (0, 2):
                    at = line * 16 + a * 4 + b
                    both = full[a * 64 : (a + 1) * 64, b * 64 : b * 64 + LANES]
                    left_ref[pair_ref[at]] += both
                    right_ref[pair_ref[at + 1]] += both
        return carry

    lax.fori_loop(0, lines // chunk, body, 0)
    left_lanes = lax.broadcasted_iota(jnp.int32, (8, 64, LANES), 2) < 64

    def emit(base):
        low, high = pl.ds(base, 8), pl.ds(base + 8, 8)
        crossed = jnp.where(left_lanes, left_ref[high], right_ref[low])
        return jnp.where(left_lanes, left_ref[low], right_ref[high]) + pltpu.roll(crossed, 64, 2)

    kept = keep_ref.shape[0] // 8
    given = give_ref.shape[0] // 8
    copies = []
    for i in range(given):
        give_ref[i * 8 : i * 8 + 8] = emit(base_ref[kept + i]).astype(BF16)
        target = first_hbm.at[pl.ds(i * 8, 8)] if i < 3 else rest_hbm.at[pl.ds(i * 8 - 24, 8)]
        copies.append(pltpu.make_async_copy(give_ref.at[pl.ds(i * 8, 8)], target, out_sems.at[kept + i]))
        copies[-1].start()
    for i in range(kept):
        keep_ref[i * 8 : i * 8 + 8] = emit(base_ref[i])
        copies.append(pltpu.make_async_copy(keep_ref.at[pl.ds(i * 8, 8)], keep_hbm.at[pl.ds(i * 8, 8)], out_sems.at[i]))
        copies[-1].start()
    for copy in copies:
        copy.wait()


def per_device(orbitals, live_atoms, pair_index, density_blocks):
    cells_x, cells_z, width, line_cells = orbitals.shape
    cols = lax.axis_size("col")
    heights = lax.axis_size("height")
    full_x = cells_x * cols
    full_z = cells_z * heights
    lines = cells_x * cells_z
    share = density_blocks.shape[0]
    devices = cols * heights
    copies = devices // line_cells
    chunk = 16
    block_rows = share * heights // 2

    cas_y = cas_table(line_cells)
    cas_y2 = np.repeat(cas_y, copies, axis=1)
    cas_x = cas_table(full_x)
    order = np.arange(full_x).reshape(cols, cells_x).T.reshape(-1)
    half_x = full_x // copies
    forward_x = cas_x.reshape(copies, half_x, full_x)[:, :, order]
    back_x = forward_x.transpose(0, 2, 1).copy()
    cas_z = cas_table(full_z)
    norm = 1.0 / (full_x * full_z * line_cells)
    unit = FOUR_PI * norm
    sym_x = np.broadcast_to(symbol(full_x).reshape(copies, half_x, 1) / unit, (copies, half_x, LANES)).astype(np.float32)
    sym_z = ((symbol(full_z) + KAPPA * KAPPA) / unit).reshape(1, full_z).astype(np.float32)
    sym_y = (symbol(line_cells) / unit).astype(np.float32)

    orb = orbitals.reshape(lines, width, line_cells)
    live = live_atoms.reshape(lines)
    pairs = pair_index.reshape(lines * 16)
    packed = jnp.concatenate([density_blocks[: share // 2], density_blocks[share // 2 :]], axis=2)
    chips = heights // 2
    far = chips // 2
    height = lax.axis_index("height")
    chip, core = height // 2, height % 2
    turn = 1 - 2 * core
    twin = [(h, h ^ 1) for h in range(heights)]

    def across(values):
        return lax.ppermute(values, "height", twin)

    def onward(values, hops):
        shift = 2 * hops
        return lax.ppermute(values, "height", [(h, (h + shift * (1 - 2 * (h % 2))) % heights) for h in range(heights)])

    def place_of(distance, owner):
        return ((chip + distance) % chips) * 2 + owner

    whole_chip = jnp.concatenate([packed, across(packed)], axis=0)
    near = onward(whole_chip, 1)
    second = onward(whole_chip, 2)
    arrived = [near, second, onward(near, 2), onward(second[: share // 2], 2)]
    pieces = [whole_chip]
    heights_of = [place_of(0, core), place_of(0, 1 - core)]
    for d, piece in enumerate(arrived, 1):
        pieces += [piece, across(piece)]
        count = 2 if d < far else 1
        heights_of += [place_of(-turn * d, core), place_of(-turn * d, 1 - core)][:count]
        heights_of += [place_of(turn * d, 1 - core), place_of(turn * d, core)][:count]
    table_rows = (jnp.stack(heights_of) * (share // 2)).astype(jnp.int32)
    keep_of, give_of = [], []
    for d in range(far, -1, -1):
        keep_of.append(place_of(turn * d, core))
        give_of.append(place_of(-turn * d, 1 - core))
        if 0 < d < far:
            keep_of.append(place_of(turn * d, 1 - core))
            give_of.append(place_of(-turn * d, core))
    sum_rows = (jnp.stack(keep_of + give_of) * share).astype(jnp.int32)

    side = jnp.arange(lines * 16, dtype=jnp.int32) % 2
    table_index = (pairs // share) * (share // 2) + pairs % (share // 2)
    table_index = table_index + jnp.where((pairs // (share // 2)) % 2 == side, 0, block_rows)
    smem = pl.BlockSpec(memory_space=pltpu.SMEM)
    vmem = pl.BlockSpec(memory_space=pltpu.VMEM)
    hbm = pl.BlockSpec(memory_space=pl.ANY)
    params = pltpu.CompilerParams(vmem_limit_bytes=VMEM_LIMIT)
    density, spectrum = pl.pallas_call(
        functools.partial(density_kernel, chunk=chunk),
        in_specs=[smem, smem, smem, hbm] + [hbm] * len(pieces) + [vmem],
        out_specs=[vmem, vmem],
        out_shape=[
            jax.ShapeDtypeStruct((lines, line_cells), F32),
            jax.ShapeDtypeStruct((devices, LANES), F32),
        ],
        scratch_shapes=[
            pltpu.VMEM((lines, width, line_cells), BF16),
            pltpu.VMEM((2 * block_rows, 64, LANES), BF16),
            pltpu.SemaphoreType.DMA((lines // chunk,)),
            pltpu.SemaphoreType.DMA((heights,)),
        ],
        compiler_params=params,
        name="density",
    )(table_index, live, table_rows, orb, *pieces, jnp.asarray(cas_y2))

    def exchange(values):
        out = lax.all_to_all(values.reshape(devices, 1, LANES), ("col", "height"), split_axis=0, concat_axis=0, tiled=True)
        return out.reshape(devices, LANES)

    device = lax.axis_index("col") * heights + height
    part = jnp.stack([device % copies, device // copies]).astype(jnp.int32)
    solved = pl.pallas_call(
        lambda *refs: solve_kernel(*refs, cells_x=cells_x, cells_z=cells_z, cols=cols, heights=heights),
        in_specs=[smem, vmem, vmem, vmem, vmem, vmem, vmem, smem],
        out_specs=vmem,
        out_shape=jax.ShapeDtypeStruct((devices, LANES), F32),
        compiler_params=params,
        name="solve",
    )(
        part,
        exchange(spectrum),
        jnp.asarray(forward_x),
        jnp.asarray(back_x),
        jnp.asarray(cas_z),
        jnp.asarray(sym_x),
        jnp.asarray(sym_z),
        jnp.asarray(sym_y),
    )
    returned = exchange(solved)

    half_rows = block_rows // 2
    potential, keep, give_first, give_rest = pl.pallas_call(
        functools.partial(hamiltonian_kernel, chunk=chunk),
        in_specs=[smem, smem, smem, hbm, vmem, vmem, vmem],
        out_specs=[vmem, hbm, hbm, hbm],
        out_shape=[
            jax.ShapeDtypeStruct((lines, line_cells), F32),
            jax.ShapeDtypeStruct((half_rows, 64, LANES), F32),
            jax.ShapeDtypeStruct((3 * share // 2, 64, LANES), BF16),
            jax.ShapeDtypeStruct((half_rows - 3 * share // 2, 64, LANES), BF16),
        ],
        scratch_shapes=[
            pltpu.VMEM((lines, width, line_cells), BF16),
            pltpu.VMEM((2 * block_rows, 64, LANES), F32),
            pltpu.VMEM((2 * block_rows, 64, LANES), F32),
            pltpu.VMEM((half_rows, 64, LANES), F32),
            pltpu.VMEM((half_rows, 64, LANES), BF16),
            pltpu.SemaphoreType.DMA((lines // chunk,)),
            pltpu.SemaphoreType.DMA((heights,)),
        ],
        compiler_params=params,
        name="hamiltonian",
    )(pairs, live, sum_rows, orb, density, returned, jnp.asarray(cas_y2.T.copy()))

    half = share // 2
    got_first = across(give_first)
    got_rest = across(lax.optimization_barrier((give_rest, got_first))[0])
    inner = onward((keep[: 3 * half] + got_first.astype(F32)).astype(BF16), 2)
    local = keep[3 * half :] + got_rest.astype(F32)
    from_far = jnp.concatenate([inner[:half].astype(F32), jnp.zeros((half, 64, LANES), F32)], axis=0)
    by_two = onward((local[: 2 * half] + from_far).astype(BF16), 2)
    by_one = onward((local[2 * half : 4 * half] + inner[half:].astype(F32)).astype(BF16), 1)
    summed = local[4 * half :] + by_two[:half].astype(F32) + by_one[:half].astype(F32)
    summed = summed + across(by_two[half:]).astype(F32) + across(by_one[half:]).astype(F32)
    hamiltonian = jnp.concatenate([summed[:, :, :64], summed[:, :, 64:]], axis=0)
    return potential.reshape(cells_x, cells_z, line_cells), hamiltonian


def solution(mesh):
    placed = (
        P("col", "height", None, None),
        P("col", "height"),
        P("col", "height", None, None),
        P(("col", "height"), None, None),
    )
    return jax.shard_map(
        per_device,
        mesh=mesh,
        in_specs=placed,
        out_specs=(P("col", "height", None), P(("col", "height"), None, None)),
        check_vma=False,
    )
```

```python
import functools

import jax
import jax.numpy as jnp
import numpy as np
from jax import lax
from jax.experimental import pallas as pl
from jax.experimental.pallas import tpu as pltpu
from jax.sharding import PartitionSpec as P

XC_COEF = 0.7386
FOUR_PI = 12.566370614359172
KAPPA = 0.5
LANES = 128
F32 = jnp.float32
BF16 = jnp.bfloat16
HIGHEST = lax.Precision.HIGHEST
VMEM_LIMIT = 32 * 1024 * 1024


def cas_table(count):
    steps = np.arange(count)
    angle = 2.0 * np.pi * (steps[:, None] * steps[None, :] % count) / count
    return (np.cos(angle) + np.sin(angle)).astype(np.float32)


def symbol(count):
    return (2.0 - 2.0 * np.cos(2.0 * np.pi * np.arange(count) / count)).astype(np.float32)


def masked_line(orb_ref, line, live):
    parts = []
    for a in range(4):
        rows = orb_ref[line, a * 64 : (a + 1) * 64, :]
        parts.append(rows if a == 0 else jnp.where(a < live, rows, jnp.zeros((), BF16)))
    return jnp.concatenate(parts, axis=0)


def density_kernel(index_ref, live_ref, part_ref, base_ref, orb_hbm, *refs, chunk):
    pieces, (cas_ref, dens_ref, spec_ref, table_ref, orb_ref, sems) = refs[:-6], refs[-6:]
    packed_rows = table_ref.shape[0] // 2

    def fetch(i):
        rows = pl.ds(i * chunk, chunk)
        return pltpu.make_async_copy(orb_hbm.at[rows], orb_ref.at[rows], sems.at[i])

    for i in range(orb_ref.shape[0] // chunk):
        fetch(i).start()
    at = 0
    for piece in pieces:
        for first in range(0, piece.shape[0], 8):
            base = base_ref[part_ref[2], at]
            at += 1
            both = piece[first : first + 8]
            table_ref[pl.ds(base, 8)] = both
            table_ref[pl.ds(packed_rows + base, 8)] = pltpu.roll(both, 64, 2)
    left_lanes = lax.broadcasted_iota(jnp.int32, (64, LANES), 1) < 64

    def body(i, carry):
        first = i * chunk
        fetch(i).wait()
        rows_out = []
        for l in range(chunk):
            line = first + l
            phi = masked_line(orb_ref, line, live_ref[line])
            strips = []
            for a in range(4):
                halves = []
                for b in (0, 2):
                    at = line * 16 + a * 4 + b
                    halves.append(jnp.where(left_lanes, table_ref[index_ref[at]], table_ref[index_ref[at + 1]]))
                strips.append(jnp.concatenate(halves, axis=1))
            matrix = jnp.concatenate(strips, axis=0)
            product = jnp.dot(matrix, phi, preferred_element_type=F32)
            rows_out.append(jnp.sum(phi.astype(F32) * product, axis=0, keepdims=True))
        dens_ref[pl.ds(pl.multiple_of(first, 8), chunk), :] = jnp.concatenate(rows_out, axis=0)
        return carry

    lax.fori_loop(0, orb_ref.shape[0] // chunk, body, 0)
    spectrum = jnp.dot(dens_ref[...], cas_ref[...], precision=HIGHEST, preferred_element_type=F32)
    lines = spectrum.shape[0]
    wide = jnp.concatenate([spectrum, jnp.zeros((LANES - lines, spectrum.shape[1]), F32)], axis=0)
    spec_ref[...] = wide.T


def solve_kernel(part_ref, in_ref, cx_ref, cxt_ref, cz_ref, sx_ref, sz_ref, sy_ref, out_ref, *, cells_x, cells_z, cols, heights):
    core = part_ref[0]
    plane = part_ref[1]
    lane = lax.broadcasted_iota(jnp.int32, (cols, LANES), 1)
    group_of = lane // cells_z
    slots = LANES // cells_z
    skewed = [
        pltpu.roll(in_ref[pl.ds(h, cols, stride=heights), :], cells_z * h, 1) if h else in_ref[pl.ds(h, cols, stride=heights), :]
        for h in range(heights)
    ]
    rows = []
    for x in range(cells_x):
        mixed = jnp.zeros((cols, LANES), F32)
        for g in range(slots):
            mixed = jnp.where(group_of == g, skewed[(g - x) % slots], mixed)
        rows.append(pltpu.roll(mixed, LANES - cells_z * x, 1) if x else mixed)
    field = jnp.concatenate(rows, axis=0)
    forward = cx_ref[core]
    spec = jnp.dot(forward, field, precision=HIGHEST, preferred_element_type=F32)
    spec = jnp.dot(spec, cz_ref[...], precision=HIGHEST, preferred_element_type=F32)
    scale = sx_ref[core] + sz_ref[...] + sy_ref[plane]
    spec = spec / scale
    spec = jnp.dot(spec, cz_ref[...], precision=HIGHEST, preferred_element_type=F32)
    back = jnp.dot(cxt_ref[core], spec, precision=HIGHEST, preferred_element_type=F32)
    skewed = []
    for x in range(cells_x):
        part = back[x * cols : (x + 1) * cols]
        skewed.append(pltpu.roll(part, cells_z * x, 1) if x else part)
    for h in range(heights):
        mixed = jnp.zeros((cols, LANES), F32)
        for x in range(cells_x):
            mixed = jnp.where(group_of == (h + x) % slots, skewed[x], mixed)
        mixed = pltpu.roll(mixed, LANES - cells_z * h, 1) if h else mixed
        out_ref[pl.ds(h, cols, stride=heights), :] = mixed


def hamiltonian_kernel(
    pair_ref,
    live_ref,
    part_ref,
    base_ref,
    orb_ref,
    dens_ref,
    back_ref,
    cas_ref,
    pot_ref,
    keep_ref,
    first_ref,
    rest_ref,
    left_ref,
    right_ref,
    *,
    chunk,
):
    lines = dens_ref.shape[0]

    def clear(i, carry):
        left_ref[pl.ds(i * 8, 8)] = jnp.zeros((8, 64, LANES), F32)
        right_ref[pl.ds(i * 8, 8)] = jnp.zeros((8, 64, LANES), F32)
        return carry

    lax.fori_loop(0, left_ref.shape[0] // 8, clear, 0)
    hartree = lax.dot_general(
        back_ref[...].T, cas_ref[...], (((1,), (0,)), ((), ())), precision=HIGHEST, preferred_element_type=F32
    )
    dens = dens_ref[...]
    pot_ref[...] = hartree[:lines] - XC_COEF * jnp.exp(jnp.log(dens * dens + 1.0) * (1.0 / 6.0))

    def body(i, carry):
        first = i * chunk
        potential = pot_ref[pl.ds(pl.multiple_of(first, 8), chunk), :]
        for l in range(chunk):
            line = first + l
            phi = masked_line(orb_ref, line, live_ref[line])
            weighted = (phi.astype(F32) * potential[l : l + 1, :]).astype(BF16)
            full = lax.dot_general(weighted, phi, (((1,), (1,)), ((), ())), preferred_element_type=F32)
            for a in range(4):
                for b in (0, 2):
                    at = line * 16 + a * 4 + b
                    both = full[a * 64 : (a + 1) * 64, b * 64 : b * 64 + LANES]
                    left_ref[pair_ref[at]] += both
                    right_ref[pair_ref[at + 1]] += both
        return carry

    lax.fori_loop(0, lines // chunk, body, 0)
    left_lanes = lax.broadcasted_iota(jnp.int32, (8, 64, LANES), 2) < 64

    def emit(base):
        low, high = pl.ds(base, 8), pl.ds(base + 8, 8)
        crossed = jnp.where(left_lanes, left_ref[high], right_ref[low])
        return jnp.where(left_lanes, left_ref[low], right_ref[high]) + pltpu.roll(crossed, 64, 2)

    at = 0
    for out in (keep_ref, first_ref, rest_ref):
        for first in range(0, out.shape[0], 8):
            out[first : first + 8] = emit(base_ref[part_ref[2], at]).astype(out.dtype)
            at += 1


def finish_kernel(keep_ref, got_ref, one_ref, two_ref, twin_one_ref, twin_two_ref, out_ref):
    rows = out_ref.shape[0] // 2
    for i in range(rows):
        total = keep_ref[keep_ref.shape[0] - rows + i] + got_ref[got_ref.shape[0] - rows + i].astype(F32)
        total = total + one_ref[i].astype(F32) + two_ref[i].astype(F32)
        total = total + twin_one_ref[i].astype(F32) + twin_two_ref[i].astype(F32)
        out_ref[i] = total[:, :64]
        out_ref[rows + i] = total[:, 64:]


def per_device(orbitals, live_atoms, pair_index, density_blocks):
    cells_x, cells_z, width, line_cells = orbitals.shape
    cols = lax.axis_size("col")
    heights = lax.axis_size("height")
    full_x = cells_x * cols
    full_z = cells_z * heights
    lines = cells_x * cells_z
    share = density_blocks.shape[0]
    devices = cols * heights
    copies = devices // line_cells
    chunk = 16
    block_rows = share * heights // 2

    cas_y = cas_table(line_cells)
    cas_y2 = np.repeat(cas_y, copies, axis=1)
    cas_x = cas_table(full_x)
    order = np.arange(full_x).reshape(cols, cells_x).T.reshape(-1)
    half_x = full_x // copies
    forward_x = cas_x.reshape(copies, half_x, full_x)[:, :, order]
    back_x = forward_x.transpose(0, 2, 1).copy()
    cas_z = cas_table(full_z)
    norm = 1.0 / (full_x * full_z * line_cells)
    unit = FOUR_PI * norm
    sym_x = np.broadcast_to(symbol(full_x).reshape(copies, half_x, 1) / unit, (copies, half_x, LANES)).astype(np.float32)
    sym_z = ((symbol(full_z) + KAPPA * KAPPA) / unit).reshape(1, full_z).astype(np.float32)
    sym_y = (symbol(line_cells) / unit).astype(np.float32)

    orb = orbitals.reshape(lines, width, line_cells)
    live = live_atoms.reshape(lines)
    pairs = pair_index.reshape(lines * 16)
    packed = jnp.concatenate([density_blocks[: share // 2], density_blocks[share // 2 :]], axis=2)
    chips = heights // 2
    far = chips // 2
    height = lax.axis_index("height")
    device = lax.axis_index("col") * heights + height
    part = jnp.stack([device % copies, device // copies, height]).astype(jnp.int32)
    twin = [(h, h ^ 1) for h in range(heights)]

    def across(values):
        return lax.ppermute(values, "height", twin)

    def onward(values, hops):
        shift = 2 * hops
        return lax.ppermute(values, "height", [(h, (h + shift * (1 - 2 * (h % 2))) % heights) for h in range(heights)])

    gather_rows, keep_rows, give_rows = [], [], []
    for h in range(heights):
        core, turn = h % 2, 1 - 2 * (h % 2)

        def place_of(distance, owner):
            return ((h // 2 + distance) % chips) * 2 + owner

        places = [place_of(0, core), place_of(0, 1 - core)]
        for d in (2, 1, 3, far):
            count = 2 if d < far else 1
            places += [place_of(-turn * d, core), place_of(-turn * d, 1 - core)][:count]
            places += [place_of(turn * d, 1 - core), place_of(turn * d, core)][:count]
        gather_rows.append(places)
        keep, give = [], []
        for d in (far, 3, 1, 2, 0):
            count = 2 if 0 < d < far else 1
            keep += [place_of(turn * d, core), place_of(turn * d, 1 - core)][:count]
            give += [place_of(-turn * d, 1 - core), place_of(-turn * d, core)][:count]
        keep_rows.append(keep)
        give_rows.append(give)
    half = share // 2
    table_rows = np.array(gather_rows, np.int32) * half
    sum_rows = np.concatenate([np.array(keep_rows, np.int32), np.array(give_rows, np.int32)], axis=1) * share

    side = jnp.arange(lines * 16, dtype=jnp.int32) % 2
    table_index = (pairs // share) * half + pairs % half
    table_index = table_index + jnp.where((pairs // half) % 2 == side, 0, block_rows)
    whole_chip = jnp.concatenate([packed, across(packed)], axis=0)
    second = onward(whole_chip, 2)
    near = onward(whole_chip, 1)
    near, table_index, live, part, pairs = lax.optimization_barrier((near, table_index, live, part, pairs))
    pieces = [whole_chip]
    for piece in (second, near, onward(second, 1), onward(second[:half], 2)):
        pieces += [piece, across(piece)]
    smem = pl.BlockSpec(memory_space=pltpu.SMEM)
    vmem = pl.BlockSpec(memory_space=pltpu.VMEM)
    params = pltpu.CompilerParams(vmem_limit_bytes=VMEM_LIMIT)
    density, spectrum = pl.pallas_call(
        functools.partial(density_kernel, chunk=chunk),
        in_specs=[smem] * 4 + [pl.BlockSpec(memory_space=pl.ANY)] + [vmem] * (len(pieces) + 1),
        out_specs=[vmem, vmem],
        out_shape=[
            jax.ShapeDtypeStruct((lines, line_cells), F32),
            jax.ShapeDtypeStruct((devices, LANES), F32),
        ],
        scratch_shapes=[
            pltpu.VMEM((2 * block_rows, 64, LANES), BF16),
            pltpu.VMEM((lines, width, line_cells), BF16),
            pltpu.SemaphoreType.DMA((lines // chunk,)),
        ],
        compiler_params=params,
        name="density",
    )(table_index, live, part, jnp.asarray(table_rows), orb, *pieces, jnp.asarray(cas_y2))

    def exchange(values):
        out = lax.all_to_all(values.reshape(devices, 1, LANES), ("col", "height"), split_axis=0, concat_axis=0, tiled=True)
        return out.reshape(devices, LANES)

    solved = pl.pallas_call(
        lambda *refs: solve_kernel(*refs, cells_x=cells_x, cells_z=cells_z, cols=cols, heights=heights),
        in_specs=[smem, vmem, vmem, vmem, vmem, vmem, vmem, smem],
        out_specs=vmem,
        out_shape=jax.ShapeDtypeStruct((devices, LANES), F32),
        compiler_params=params,
        name="solve",
    )(
        part,
        exchange(spectrum),
        jnp.asarray(forward_x),
        jnp.asarray(back_x),
        jnp.asarray(cas_z),
        jnp.asarray(sym_x),
        jnp.asarray(sym_z),
        jnp.asarray(sym_y),
    )
    returned = exchange(solved)

    half_rows = block_rows // 2
    potential, keep, give_first, give_rest = pl.pallas_call(
        functools.partial(hamiltonian_kernel, chunk=chunk),
        in_specs=[smem] * 4 + [vmem] * 4,
        out_specs=[vmem] * 4,
        out_shape=[
            jax.ShapeDtypeStruct((lines, line_cells), F32),
            jax.ShapeDtypeStruct((half_rows, 64, LANES), F32),
            jax.ShapeDtypeStruct((3 * share // 2, 64, LANES), BF16),
            jax.ShapeDtypeStruct((half_rows - 3 * share // 2, 64, LANES), BF16),
        ],
        scratch_shapes=[pltpu.VMEM((2 * block_rows, 64, LANES), F32)] * 2,
        compiler_params=params,
        name="hamiltonian",
    )(pairs, live, part, jnp.asarray(sum_rows), orb, density, returned, jnp.asarray(cas_y2.T.copy()))

    got_first = across(give_first)
    got_rest = across(lax.optimization_barrier((give_rest, got_first))[0])
    begin = (keep[: 3 * half] + got_first.astype(F32)).astype(BF16)
    from_far = onward(begin[:half], 2).astype(F32)
    from_third = onward(begin[half:], 1).astype(F32)
    local = keep[3 * half :] + got_rest.astype(F32)
    by_one = onward(local[: 2 * half].astype(BF16), 1)
    from_far = jnp.concatenate([from_far, jnp.zeros_like(from_far)], axis=0)
    by_two = onward((local[2 * half : 4 * half] + from_third + from_far).astype(BF16), 2)
    hamiltonian = pl.pallas_call(
        finish_kernel,
        in_specs=[vmem] * 6,
        out_specs=vmem,
        out_shape=jax.ShapeDtypeStruct(density_blocks.shape, F32),
        compiler_params=params,
        name="finish",
    )(keep, got_rest, by_one, by_two, across(by_one[half:]), across(by_two[half:]))
    return potential.reshape(cells_x, cells_z, line_cells), hamiltonian


def solution(mesh):
    placed = (
        P("col", "height", None, None),
        P("col", "height"),
        P("col", "height", None, None),
        P(("col", "height"), None, None),
    )
    return jax.shard_map(
        per_device,
        mesh=mesh,
        in_specs=placed,
        out_specs=(P("col", "height", None), P(("col", "height"), None, None)),
        check_vma=False,
    )
```

```python
import functools

import jax
import jax.numpy as jnp
import numpy as np
from jax import lax
from jax.experimental import pallas as pl
from jax.experimental.pallas import tpu as pltpu
from jax.sharding import PartitionSpec as P

XC_COEF = 0.7386
FOUR_PI = 12.566370614359172
KAPPA = 0.5
LANES = 128
F32 = jnp.float32
BF16 = jnp.bfloat16
HIGHEST = lax.Precision.HIGHEST
VMEM_LIMIT = 12 * 1024 * 1024
STAGE_LIMIT = 12 * 1024 * 1024


def cas_table(count):
    steps = np.arange(count)
    angle = 2.0 * np.pi * (steps[:, None] * steps[None, :] % count) / count
    return (np.cos(angle) + np.sin(angle)).astype(np.float32)


def symbol(count):
    return (2.0 - 2.0 * np.cos(2.0 * np.pi * np.arange(count) / count)).astype(np.float32)


def block_base(height, chips, share, place):
    distance, flip = place
    core = lax.rem(height, 2)
    chip = lax.rem(height // 2 + distance * (1 - 2 * core) + chips, chips)
    return (chip * 2 + (1 - core if flip else core)) * share


def masked_line(orb_ref, line, live):
    parts = []
    for a in range(4):
        rows = orb_ref[line, a * 64 : (a + 1) * 64, :]
        parts.append(rows if a == 0 else jnp.where(a < live, rows, jnp.zeros((), BF16)))
    return jnp.concatenate(parts, axis=0)


def stage_kernel(orb_hbm, orb_ref, left_ref, right_ref, sem):
    copy = pltpu.make_async_copy(orb_hbm, orb_ref, sem)
    copy.start()

    def clear(i, carry):
        left_ref[pl.ds(i * 8, 8)] = jnp.zeros((8, 64, LANES), F32)
        right_ref[pl.ds(i * 8, 8)] = jnp.zeros((8, 64, LANES), F32)
        return carry

    lax.fori_loop(0, left_ref.shape[0] // 8, clear, 0)
    copy.wait()


def density_kernel(index_ref, live_ref, part_ref, orb_ref, *refs, chunk, places, chips):
    pieces, (cas_ref, dens_ref, spec_ref, table_ref) = refs[:-4], refs[-4:]
    packed_rows = table_ref.shape[0] // 2

    at = 0
    for piece in pieces:
        for first in range(0, piece.shape[0], 8):
            base = block_base(part_ref[2], chips, 8, places[at])
            at += 1
            both = piece[first : first + 8]
            table_ref[pl.ds(base, 8)] = both
            table_ref[pl.ds(packed_rows + base, 8)] = pltpu.roll(both, 64, 2)
    left_lanes = lax.broadcasted_iota(jnp.int32, (64, LANES), 1) < 64

    def body(i, carry):
        first = i * chunk
        rows_out = []
        for l in range(chunk):
            line = first + l
            phi = masked_line(orb_ref, line, live_ref[line])
            strips = []
            for a in range(4):
                halves = []
                for b in (0, 2):
                    at = line * 16 + a * 4 + b
                    halves.append(jnp.where(left_lanes, table_ref[index_ref[at]], table_ref[index_ref[at + 1]]))
                strips.append(jnp.concatenate(halves, axis=1))
            matrix = jnp.concatenate(strips, axis=0)
            product = jnp.dot(matrix, phi, preferred_element_type=F32)
            rows_out.append(jnp.sum(phi.astype(F32) * product, axis=0, keepdims=True))
        dens_ref[pl.ds(pl.multiple_of(first, 8), chunk), :] = jnp.concatenate(rows_out, axis=0)
        return carry

    lax.fori_loop(0, orb_ref.shape[0] // chunk, body, 0)
    spectrum = jnp.dot(dens_ref[...], cas_ref[...], precision=HIGHEST, preferred_element_type=F32)
    lines = spectrum.shape[0]
    wide = jnp.concatenate([spectrum, jnp.zeros((LANES - lines, spectrum.shape[1]), F32)], axis=0)
    spec_ref[...] = wide.T


def solve_kernel(part_ref, in_ref, cx_ref, cxt_ref, cz_ref, sx_ref, sz_ref, sy_ref, out_ref, *, cells_x, cells_z, cols, heights):
    core = part_ref[0]
    plane = part_ref[1]
    lane = lax.broadcasted_iota(jnp.int32, (cols, LANES), 1)
    group_of = lane // cells_z
    slots = LANES // cells_z
    skewed = [
        pltpu.roll(in_ref[pl.ds(h, cols, stride=heights), :], cells_z * h, 1) if h else in_ref[pl.ds(h, cols, stride=heights), :]
        for h in range(heights)
    ]
    rows = []
    for x in range(cells_x):
        mixed = jnp.zeros((cols, LANES), F32)
        for g in range(slots):
            mixed = jnp.where(group_of == g, skewed[(g - x) % slots], mixed)
        rows.append(pltpu.roll(mixed, LANES - cells_z * x, 1) if x else mixed)
    field = jnp.concatenate(rows, axis=0)
    forward = cx_ref[core]
    spec = jnp.dot(forward, field, precision=HIGHEST, preferred_element_type=F32)
    spec = jnp.dot(spec, cz_ref[...], precision=HIGHEST, preferred_element_type=F32)
    scale = sx_ref[core] + sz_ref[...] + sy_ref[plane]
    spec = spec / scale
    spec = jnp.dot(spec, cz_ref[...], precision=HIGHEST, preferred_element_type=F32)
    back = jnp.dot(cxt_ref[core], spec, precision=HIGHEST, preferred_element_type=F32)
    skewed = []
    for x in range(cells_x):
        part = back[x * cols : (x + 1) * cols]
        skewed.append(pltpu.roll(part, cells_z * x, 1) if x else part)
    for h in range(heights):
        mixed = jnp.zeros((cols, LANES), F32)
        for x in range(cells_x):
            mixed = jnp.where(group_of == (h + x) % slots, skewed[x], mixed)
        mixed = pltpu.roll(mixed, LANES - cells_z * h, 1) if h else mixed
        out_ref[pl.ds(h, cols, stride=heights), :] = mixed


def hamiltonian_kernel(
    pair_ref,
    live_ref,
    part_ref,
    orb_ref,
    dens_ref,
    back_ref,
    cas_ref,
    left_in,
    right_in,
    pot_ref,
    keep_ref,
    first_ref,
    rest_ref,
    left_ref,
    right_ref,
    *,
    chunk,
    places,
    chips,
):
    lines = dens_ref.shape[0]

    hartree = jnp.dot(cas_ref[...], back_ref[...], precision=HIGHEST, preferred_element_type=F32).T
    dens = dens_ref[...]
    pot_ref[...] = hartree[:lines] - XC_COEF * jnp.exp(jnp.log(dens * dens + 1.0) * (1.0 / 6.0))

    def body(i, carry):
        first = i * chunk
        potential = pot_ref[pl.ds(pl.multiple_of(first, 8), chunk), :]
        for l in range(chunk):
            line = first + l
            phi = masked_line(orb_ref, line, live_ref[line])
            weighted = (phi.astype(F32) * potential[l : l + 1, :]).astype(BF16)
            full = lax.dot_general(weighted, phi, (((1,), (1,)), ((), ())), preferred_element_type=F32)
            for a in range(4):
                for b in (0, 2):
                    at = line * 16 + a * 4 + b
                    both = full[a * 64 : (a + 1) * 64, b * 64 : b * 64 + LANES]
                    left_ref[pair_ref[at]] += both
                    right_ref[pair_ref[at + 1]] += both
        return carry

    lax.fori_loop(0, lines // chunk, body, 0)
    left_lanes = lax.broadcasted_iota(jnp.int32, (8, 64, LANES), 2) < 64

    def emit(base):
        low, high = pl.ds(base, 8), pl.ds(base + 8, 8)
        crossed = jnp.where(left_lanes, left_ref[high], right_ref[low])
        return jnp.where(left_lanes, left_ref[low], right_ref[high]) + pltpu.roll(crossed, 64, 2)

    at = 0
    for out in (keep_ref, first_ref, rest_ref):
        for first in range(0, out.shape[0], 8):
            out[first : first + 8] = emit(block_base(part_ref[2], chips, 16, places[at])).astype(out.dtype)
            at += 1


def finish_kernel(keep_ref, got_ref, one_ref, two_ref, twin_one_ref, twin_two_ref, out_ref):
    rows = out_ref.shape[0] // 2
    for i in range(rows):
        total = keep_ref[keep_ref.shape[0] - rows + i] + got_ref[got_ref.shape[0] - rows + i].astype(F32)
        total = total + one_ref[i].astype(F32) + two_ref[i].astype(F32)
        total = total + twin_one_ref[i].astype(F32) + twin_two_ref[i].astype(F32)
        out_ref[i] = total[:, :64]
        out_ref[rows + i] = total[:, 64:]


def per_device(orbitals, live_atoms, pair_index, density_blocks):
    cells_x, cells_z, width, line_cells = orbitals.shape
    cols = lax.axis_size("col")
    heights = lax.axis_size("height")
    full_x = cells_x * cols
    full_z = cells_z * heights
    lines = cells_x * cells_z
    share = density_blocks.shape[0]
    devices = cols * heights
    copies = devices // line_cells
    chunk = 16
    block_rows = share * heights // 2

    cas_y = cas_table(line_cells)
    cas_y2 = np.repeat(cas_y, copies, axis=1)
    cas_x = cas_table(full_x)
    order = np.arange(full_x).reshape(cols, cells_x).T.reshape(-1)
    half_x = full_x // copies
    forward_x = cas_x.reshape(copies, half_x, full_x)[:, :, order]
    back_x = forward_x.transpose(0, 2, 1).copy()
    cas_z = cas_table(full_z)
    norm = 1.0 / (full_x * full_z * line_cells)
    unit = FOUR_PI * norm
    sym_x = np.broadcast_to(symbol(full_x).reshape(copies, half_x, 1) / unit, (copies, half_x, LANES)).astype(np.float32)
    sym_z = ((symbol(full_z) + KAPPA * KAPPA) / unit).reshape(1, full_z).astype(np.float32)
    sym_y = (symbol(line_cells) / unit).astype(np.float32)

    orb = orbitals.reshape(lines, width, line_cells)
    live = live_atoms.reshape(lines)
    pairs = pair_index.reshape(lines * 16)
    packed = jnp.concatenate([density_blocks[: share // 2], density_blocks[share // 2 :]], axis=2)
    chips = heights // 2
    far = chips // 2
    height = lax.axis_index("height")
    device = lax.axis_index("col") * heights + height
    part = jnp.stack([device % copies, device // copies, height]).astype(jnp.int32)
    twin = [(h, h ^ 1) for h in range(heights)]

    def across(values):
        return lax.ppermute(values, "height", twin)

    def onward(values, hops, sign=1, flip=0):
        def target(h):
            core = h % 2
            return (h // 2 + sign * hops * (1 - 2 * core)) % chips * 2 + (core ^ flip)

        return lax.ppermute(values, "height", [(h, target(h)) for h in range(heights)])

    half = share // 2
    gather_places = [(0, 0), (0, 1)]
    for d in (2, 1, 3):
        gather_places += [(-d, 0), (-d, 1), (d, 1), (d, 0)]
    gather_places += [(far, 0), (far, 1)]
    keep_places, give_places = [(far, 0)], [(far, 1)]
    for d in (3, 1, 2):
        keep_places += [(d, 0), (d, 1)]
        give_places += [(-d, 1), (-d, 0)]
    sum_places = keep_places + [(0, 0)] + give_places + [(0, 1)]

    side = jnp.arange(lines * 16, dtype=jnp.int32) % 2
    table_index = (pairs // share) * half + pairs % half
    table_index = table_index + jnp.where((pairs // half) % 2 == side, 0, block_rows)
    whole_chip = jnp.concatenate([packed, across(packed)], axis=0)
    second = onward(whole_chip, 2)
    near = onward(whole_chip, 1)
    smem = pl.BlockSpec(memory_space=pltpu.SMEM)
    vmem = pl.BlockSpec(memory_space=pltpu.VMEM)
    params = pltpu.CompilerParams(vmem_limit_bytes=VMEM_LIMIT)
    sums_shape = jax.ShapeDtypeStruct((2 * block_rows, 64, LANES), F32)
    orb, left, right = pl.pallas_call(
        stage_kernel,
        in_specs=[pl.BlockSpec(memory_space=pl.ANY)],
        out_specs=[vmem] * 3,
        out_shape=[jax.ShapeDtypeStruct(orb.shape, BF16), sums_shape, sums_shape],
        scratch_shapes=[pltpu.SemaphoreType.DMA(())],
        compiler_params=pltpu.CompilerParams(vmem_limit_bytes=STAGE_LIMIT),
        name="stage",
    )(orb)
    second, near, table_index, live, part, pairs, orb, left, right = lax.optimization_barrier(
        (second, near, table_index, live, part, pairs, orb, left, right)
    )
    pieces = [whole_chip]
    for piece in (second, near, onward(second, 1), onward(second[:half], 2)):
        pieces += [piece, across(piece)]
    density, spectrum = pl.pallas_call(
        functools.partial(density_kernel, chunk=chunk, places=gather_places, chips=chips),
        in_specs=[smem] * 3 + [vmem] * (len(pieces) + 2),
        out_specs=[vmem, vmem],
        out_shape=[
            jax.ShapeDtypeStruct((lines, line_cells), F32),
            jax.ShapeDtypeStruct((devices, LANES), F32),
        ],
        scratch_shapes=[pltpu.VMEM((2 * block_rows, 64, LANES), BF16)],
        compiler_params=params,
        name="density",
    )(table_index, live, part, orb, *pieces, jnp.asarray(cas_y2))

    def exchange(values):
        out = lax.all_to_all(values.reshape(devices, 1, LANES), ("col", "height"), split_axis=0, concat_axis=0, tiled=True)
        return out.reshape(devices, LANES)

    solved = pl.pallas_call(
        lambda *refs: solve_kernel(*refs, cells_x=cells_x, cells_z=cells_z, cols=cols, heights=heights),
        in_specs=[smem, vmem, vmem, vmem, vmem, vmem, vmem, smem],
        out_specs=vmem,
        out_shape=jax.ShapeDtypeStruct((devices, LANES), F32),
        compiler_params=params,
        name="solve",
    )(
        part,
        exchange(spectrum),
        jnp.asarray(forward_x),
        jnp.asarray(back_x),
        jnp.asarray(cas_z),
        jnp.asarray(sym_x),
        jnp.asarray(sym_z),
        jnp.asarray(sym_y),
    )
    returned = exchange(solved)

    half_rows = block_rows // 2
    potential, keep, give_first, give_rest, _, _ = pl.pallas_call(
        functools.partial(hamiltonian_kernel, chunk=chunk, places=sum_places, chips=chips),
        in_specs=[smem] * 3 + [vmem] * 6,
        out_specs=[vmem] * 6,
        out_shape=[
            jax.ShapeDtypeStruct((lines, line_cells), F32),
            jax.ShapeDtypeStruct((half_rows, 64, LANES), F32),
            jax.ShapeDtypeStruct((3 * share // 2, 64, LANES), BF16),
            jax.ShapeDtypeStruct((half_rows - 3 * share // 2, 64, LANES), BF16),
            sums_shape,
            sums_shape,
        ],
        input_output_aliases={7: 4, 8: 5},
        compiler_params=params,
        name="hamiltonian",
    )(pairs, live, part, orb, density, returned, jnp.asarray(cas_y2), left, right)

    got_first = across(give_first)
    got_rest = across(lax.optimization_barrier((give_rest, got_first))[0])

    def local(kept, i):
        got = got_first[i * half : (i + 1) * half] if i < 3 else got_rest[(i - 3) * half : (i - 2) * half]
        return kept[i * half : (i + 1) * half] + got.astype(F32)

    begin = lax.optimization_barrier((keep, *[local(keep, i).astype(BF16) for i in range(3)]))
    far_sum = onward(begin[1], 2)
    third = onward(begin[2], 1)
    third_twin = onward(begin[3], 1)
    ones = lax.optimization_barrier((begin[0], local(begin[0], 3).astype(BF16), local(begin[0], 4).astype(BF16)))
    by_one = onward(ones[1], 1)
    by_one_twin = onward(ones[2], 1, 1, 1)
    twos = lax.optimization_barrier((ones[0], (local(ones[0], 6) + third_twin.astype(F32)).astype(BF16)))
    by_two_twin = onward(twos[1], 2, 1, 1)
    by_two = onward((local(twos[0], 5) + far_sum.astype(F32) + third.astype(F32)).astype(BF16), 2)
    hamiltonian = pl.pallas_call(
        finish_kernel,
        in_specs=[vmem] * 6,
        out_specs=vmem,
        out_shape=jax.ShapeDtypeStruct(density_blocks.shape, F32),
        compiler_params=params,
        name="finish",
    )(keep, got_rest, by_one, by_two, by_one_twin, by_two_twin)
    return potential.reshape(cells_x, cells_z, line_cells), hamiltonian


def solution(mesh):
    placed = (
        P("col", "height", None, None),
        P("col", "height"),
        P("col", "height", None, None),
        P(("col", "height"), None, None),
    )
    return jax.shard_map(
        per_device,
        mesh=mesh,
        in_specs=placed,
        out_specs=(P("col", "height", None), P(("col", "height"), None, None)),
        check_vma=False,
    )
```

```python
import functools

import jax
import jax.numpy as jnp
import numpy as np
from jax import lax
from jax.experimental import pallas as pl
from jax.experimental.pallas import tpu as pltpu
from jax.sharding import PartitionSpec as P

XC_COEF = 0.7386
FOUR_PI = 12.566370614359172
KAPPA = 0.5
LANES = 128
F32 = jnp.float32
BF16 = jnp.bfloat16
HIGHEST = lax.Precision.HIGHEST
VMEM_LIMIT = 12 * 1024 * 1024
SUMS_LIMIT = 24 * 1024 * 1024
LINES_AT_ONCE = 8


def cas_table(count):
    steps = np.arange(count)
    angle = 2.0 * np.pi * (steps[:, None] * steps[None, :] % count) / count
    return (np.cos(angle) + np.sin(angle)).astype(np.float32)


def symbol(count):
    return (2.0 - 2.0 * np.cos(2.0 * np.pi * np.arange(count) / count)).astype(np.float32)


def block_base(height, chips, share, place):
    distance, flip = place
    core = lax.rem(height, 2)
    chip = lax.rem(height // 2 + distance * (1 - 2 * core) + chips, chips)
    return (chip * 2 + (1 - core if flip else core)) * share


def masked_line(orb_ref, line, live):
    parts = []
    for a in range(4):
        rows = orb_ref[line, a * 64 : (a + 1) * 64, :]
        parts.append(rows if a == 0 else jnp.where(a < live, rows, jnp.zeros((), BF16)))
    return jnp.concatenate(parts, axis=0)


def stage_kernel(live_ref, orb_hbm, orb_ref, order_ref, count_ref, sem):
    copy = pltpu.make_async_copy(orb_hbm, orb_ref, sem)
    copy.start()
    lines = orb_ref.shape[0]
    for n in range(4):
        count_ref[n] = 0

    def place(line, carry):
        n = live_ref[line] - 1
        order_ref[n, count_ref[n]] = line
        count_ref[n] += 1
        return carry

    lax.fori_loop(0, lines, place, 0)
    for n in range(4):
        for i in range(LINES_AT_ONCE):
            order_ref[n, count_ref[n] + i] = lines
    copy.wait()


def density_kernel(index_ref, live_ref, part_ref, orb_ref, *refs, chunk, places, chips):
    pieces, (cas_ref, dens_ref, spec_ref, table_ref) = refs[:-4], refs[-4:]
    packed_rows = table_ref.shape[0] // 2

    at = 0
    for piece in pieces:
        for first in range(0, piece.shape[0], 8):
            base = block_base(part_ref[2], chips, 8, places[at])
            at += 1
            both = piece[first : first + 8]
            table_ref[pl.ds(base, 8)] = both
            table_ref[pl.ds(packed_rows + base, 8)] = pltpu.roll(both, 64, 2)
    left_lanes = lax.broadcasted_iota(jnp.int32, (64, LANES), 1) < 64

    def body(i, carry):
        first = i * chunk
        rows_out = []
        for l in range(chunk):
            line = first + l
            phi = masked_line(orb_ref, line, live_ref[line])
            strips = []
            for a in range(4):
                halves = []
                for b in (0, 2):
                    at = line * 16 + a * 4 + b
                    halves.append(jnp.where(left_lanes, table_ref[index_ref[at]], table_ref[index_ref[at + 1]]))
                strips.append(jnp.concatenate(halves, axis=1))
            matrix = jnp.concatenate(strips, axis=0)
            product = jnp.dot(matrix, phi, preferred_element_type=F32)
            rows_out.append(jnp.sum(phi.astype(F32) * product, axis=0, keepdims=True))
        dens_ref[pl.ds(pl.multiple_of(first, 8), chunk), :] = jnp.concatenate(rows_out, axis=0)
        return carry

    lax.fori_loop(0, orb_ref.shape[0] // chunk, body, 0)
    spectrum = jnp.dot(dens_ref[...], cas_ref[...], precision=HIGHEST, preferred_element_type=F32)
    lines = spectrum.shape[0]
    wide = jnp.concatenate([spectrum, jnp.zeros((LANES - lines, spectrum.shape[1]), F32)], axis=0)
    spec_ref[...] = wide.T


def solve_kernel(part_ref, in_ref, cx_ref, cxt_ref, cz_ref, sx_ref, sz_ref, sy_ref, out_ref, *, cells_x, cells_z, cols, heights):
    core = part_ref[0]
    plane = part_ref[1]
    lane = lax.broadcasted_iota(jnp.int32, (cols, LANES), 1)
    group_of = lane // cells_z
    slots = LANES // cells_z
    skewed = [
        pltpu.roll(in_ref[pl.ds(h, cols, stride=heights), :], cells_z * h, 1) if h else in_ref[pl.ds(h, cols, stride=heights), :]
        for h in range(heights)
    ]
    rows = []
    for x in range(cells_x):
        mixed = jnp.zeros((cols, LANES), F32)
        for g in range(slots):
            mixed = jnp.where(group_of == g, skewed[(g - x) % slots], mixed)
        rows.append(pltpu.roll(mixed, LANES - cells_z * x, 1) if x else mixed)
    field = jnp.concatenate(rows, axis=0)
    forward = cx_ref[core]
    spec = jnp.dot(forward, field, precision=HIGHEST, preferred_element_type=F32)
    spec = jnp.dot(spec, cz_ref[...], precision=HIGHEST, preferred_element_type=F32)
    scale = sx_ref[core] + sz_ref[...] + sy_ref[plane]
    spec = spec / scale
    spec = jnp.dot(spec, cz_ref[...], precision=HIGHEST, preferred_element_type=F32)
    back = jnp.dot(cxt_ref[core], spec, precision=HIGHEST, preferred_element_type=F32)
    skewed = []
    for x in range(cells_x):
        part = back[x * cols : (x + 1) * cols]
        skewed.append(pltpu.roll(part, cells_z * x, 1) if x else part)
    for h in range(heights):
        mixed = jnp.zeros((cols, LANES), F32)
        for x in range(cells_x):
            mixed = jnp.where(group_of == (h + x) % slots, skewed[x], mixed)
        mixed = pltpu.roll(mixed, LANES - cells_z * h, 1) if h else mixed
        out_ref[pl.ds(h, cols, stride=heights), :] = mixed


def hamiltonian_kernel(
    pair_ref,
    order_ref,
    count_ref,
    part_ref,
    orb_ref,
    dens_ref,
    back_ref,
    cas_ref,
    pot_ref,
    keep_ref,
    first_ref,
    rest_ref,
    left_ref,
    right_ref,
    padded_ref,
    *,
    places,
    chips,
):
    lines = dens_ref.shape[0]

    def clear(i, carry):
        left_ref[pl.ds(i * 8, 8)] = jnp.zeros((8, 64, LANES), F32)
        right_ref[pl.ds(i * 8, 8)] = jnp.zeros((8, 64, LANES), F32)
        return carry

    lax.fori_loop(0, left_ref.shape[0] // 8, clear, 0)
    hartree = jnp.dot(cas_ref[...], back_ref[...], precision=HIGHEST, preferred_element_type=F32).T
    dens = dens_ref[...]
    potential = hartree[:lines] - XC_COEF * jnp.exp(jnp.log(dens * dens + 1.0) * (1.0 / 6.0))
    pot_ref[...] = potential
    padded_ref[...] = jnp.concatenate([potential, jnp.zeros((padded_ref.shape[0] - lines, LANES), F32)], axis=0)

    for n in range(1, 5):

        def body(i, carry, n=n):
            for j in range(LINES_AT_ONCE):
                entry = order_ref[n - 1, i * LINES_AT_ONCE + j]
                line = jnp.minimum(entry, lines - 1)
                rows = orb_ref[line, : n * 64, :]
                phi = rows if n % 2 == 0 else jnp.concatenate([rows, jnp.zeros((64, LANES), BF16)], axis=0)
                weighted = (rows.astype(F32) * padded_ref[pl.ds(entry, 1), :]).astype(BF16)
                full = lax.dot_general(weighted, phi, (((1,), (1,)), ((), ())), preferred_element_type=F32)
                for a in range(n):
                    for b in range(0, n, 2):
                        at = line * 16 + a * 4 + b
                        both = full[a * 64 : (a + 1) * 64, b * 64 : b * 64 + LANES]
                        left_ref[pair_ref[at]] += both
                        if b + 1 < n:
                            right_ref[pair_ref[at + 1]] += both
            return carry

        lax.fori_loop(0, (count_ref[n - 1] + LINES_AT_ONCE - 1) // LINES_AT_ONCE, body, 0)
    left_lanes = lax.broadcasted_iota(jnp.int32, (8, 64, LANES), 2) < 64

    def emit(base):
        low, high = pl.ds(base, 8), pl.ds(base + 8, 8)
        crossed = jnp.where(left_lanes, left_ref[high], right_ref[low])
        return jnp.where(left_lanes, left_ref[low], right_ref[high]) + pltpu.roll(crossed, 64, 2)

    at = 0
    for out in (keep_ref, first_ref, rest_ref):
        for first in range(0, out.shape[0], 8):
            out[first : first + 8] = emit(block_base(part_ref[2], chips, 16, places[at])).astype(out.dtype)
            at += 1


def finish_kernel(keep_ref, got_ref, one_ref, two_ref, twin_one_ref, twin_two_ref, out_ref):
    rows = out_ref.shape[0] // 2
    for i in range(rows):
        total = keep_ref[keep_ref.shape[0] - rows + i] + got_ref[got_ref.shape[0] - rows + i].astype(F32)
        total = total + one_ref[i].astype(F32) + two_ref[i].astype(F32)
        total = total + twin_one_ref[i].astype(F32) + twin_two_ref[i].astype(F32)
        out_ref[i] = total[:, :64]
        out_ref[rows + i] = total[:, 64:]


def per_device(orbitals, live_atoms, pair_index, density_blocks):
    cells_x, cells_z, width, line_cells = orbitals.shape
    cols = lax.axis_size("col")
    heights = lax.axis_size("height")
    full_x = cells_x * cols
    full_z = cells_z * heights
    lines = cells_x * cells_z
    share = density_blocks.shape[0]
    devices = cols * heights
    copies = devices // line_cells
    chunk = 16
    block_rows = share * heights // 2

    cas_y = cas_table(line_cells)
    cas_y2 = np.repeat(cas_y, copies, axis=1)
    cas_x = cas_table(full_x)
    order = np.arange(full_x).reshape(cols, cells_x).T.reshape(-1)
    half_x = full_x // copies
    forward_x = cas_x.reshape(copies, half_x, full_x)[:, :, order]
    back_x = forward_x.transpose(0, 2, 1).copy()
    cas_z = cas_table(full_z)
    norm = 1.0 / (full_x * full_z * line_cells)
    unit = FOUR_PI * norm
    sym_x = np.broadcast_to(symbol(full_x).reshape(copies, half_x, 1) / unit, (copies, half_x, LANES)).astype(np.float32)
    sym_z = ((symbol(full_z) + KAPPA * KAPPA) / unit).reshape(1, full_z).astype(np.float32)
    sym_y = (symbol(line_cells) / unit).astype(np.float32)

    orb = orbitals.reshape(lines, width, line_cells)
    live = live_atoms.reshape(lines)
    pairs = pair_index.reshape(lines * 16)
    packed = jnp.concatenate([density_blocks[: share // 2], density_blocks[share // 2 :]], axis=2)
    chips = heights // 2
    far = chips // 2
    height = lax.axis_index("height")
    device = lax.axis_index("col") * heights + height
    part = jnp.stack([device % copies, device // copies, height]).astype(jnp.int32)
    twin = [(h, h ^ 1) for h in range(heights)]

    def across(values):
        return lax.ppermute(values, "height", twin)

    def onward(values, hops, sign=1, flip=0):
        def target(h):
            core = h % 2
            return (h // 2 + sign * hops * (1 - 2 * core)) % chips * 2 + (core ^ flip)

        return lax.ppermute(values, "height", [(h, target(h)) for h in range(heights)])

    half = share // 2
    gather_places = [(0, 0), (0, 1)]
    for d in (2, 1, 3):
        gather_places += [(-d, 0), (-d, 1), (d, 1), (d, 0)]
    gather_places += [(far, 0), (far, 1)]
    keep_places, give_places = [(far, 0)], [(far, 1)]
    for d in (3, 1, 2):
        keep_places += [(d, 0), (d, 1)]
        give_places += [(-d, 1), (-d, 0)]
    sum_places = keep_places + [(0, 0)] + give_places + [(0, 1)]

    side = jnp.arange(lines * 16, dtype=jnp.int32) % 2
    table_index = (pairs // share) * half + pairs % half
    table_index = table_index + jnp.where((pairs // half) % 2 == side, 0, block_rows)
    whole_chip = jnp.concatenate([packed, across(packed)], axis=0)
    second = onward(whole_chip, 2)
    near = onward(whole_chip, 1)
    smem = pl.BlockSpec(memory_space=pltpu.SMEM)
    vmem = pl.BlockSpec(memory_space=pltpu.VMEM)
    params = pltpu.CompilerParams(vmem_limit_bytes=VMEM_LIMIT)
    orb, order, count = pl.pallas_call(
        stage_kernel,
        in_specs=[smem, pl.BlockSpec(memory_space=pl.ANY)],
        out_specs=[vmem, smem, smem],
        out_shape=[
            jax.ShapeDtypeStruct(orb.shape, BF16),
            jax.ShapeDtypeStruct((4, lines + LINES_AT_ONCE), jnp.int32),
            jax.ShapeDtypeStruct((4,), jnp.int32),
        ],
        scratch_shapes=[pltpu.SemaphoreType.DMA(())],
        compiler_params=params,
        name="stage",
    )(live, orb)
    second, near, table_index, live, part, pairs, orb, order, count = lax.optimization_barrier(
        (second, near, table_index, live, part, pairs, orb, order, count)
    )
    pieces = [whole_chip]
    for piece in (second, near, onward(second, 1), onward(second[:half], 2)):
        pieces += [piece, across(piece)]
    density, spectrum = pl.pallas_call(
        functools.partial(density_kernel, chunk=chunk, places=gather_places, chips=chips),
        in_specs=[smem] * 3 + [vmem] * (len(pieces) + 2),
        out_specs=[vmem, vmem],
        out_shape=[
            jax.ShapeDtypeStruct((lines, line_cells), F32),
            jax.ShapeDtypeStruct((devices, LANES), F32),
        ],
        scratch_shapes=[pltpu.VMEM((2 * block_rows, 64, LANES), BF16)],
        compiler_params=params,
        name="density",
    )(table_index, live, part, orb, *pieces, jnp.asarray(cas_y2))

    def exchange(values):
        out = lax.all_to_all(values.reshape(devices, 1, LANES), ("col", "height"), split_axis=0, concat_axis=0, tiled=True)
        return out.reshape(devices, LANES)

    solved = pl.pallas_call(
        lambda *refs: solve_kernel(*refs, cells_x=cells_x, cells_z=cells_z, cols=cols, heights=heights),
        in_specs=[smem, vmem, vmem, vmem, vmem, vmem, vmem, smem],
        out_specs=vmem,
        out_shape=jax.ShapeDtypeStruct((devices, LANES), F32),
        compiler_params=params,
        name="solve",
    )(
        part,
        exchange(spectrum),
        jnp.asarray(forward_x),
        jnp.asarray(back_x),
        jnp.asarray(cas_z),
        jnp.asarray(sym_x),
        jnp.asarray(sym_z),
        jnp.asarray(sym_y),
    )
    returned = exchange(solved)

    half_rows = block_rows // 2
    potential, keep, give_first, give_rest = pl.pallas_call(
        functools.partial(hamiltonian_kernel, places=sum_places, chips=chips),
        in_specs=[smem] * 4 + [vmem] * 4,
        out_specs=[vmem] * 4,
        out_shape=[
            jax.ShapeDtypeStruct((lines, line_cells), F32),
            jax.ShapeDtypeStruct((half_rows, 64, LANES), F32),
            jax.ShapeDtypeStruct((3 * share // 2, 64, LANES), BF16),
            jax.ShapeDtypeStruct((half_rows - 3 * share // 2, 64, LANES), BF16),
        ],
        scratch_shapes=[
            pltpu.VMEM((2 * block_rows, 64, LANES), F32),
            pltpu.VMEM((2 * block_rows, 64, LANES), F32),
            pltpu.VMEM((lines + 8, LANES), F32),
        ],
        compiler_params=pltpu.CompilerParams(vmem_limit_bytes=SUMS_LIMIT),
        name="hamiltonian",
    )(pairs, order, count, part, orb, density, returned, jnp.asarray(cas_y2))

    got_first = across(give_first)
    got_rest = across(lax.optimization_barrier((give_rest, got_first))[0])

    def local(kept, i):
        got = got_first[i * half : (i + 1) * half] if i < 3 else got_rest[(i - 3) * half : (i - 2) * half]
        return kept[i * half : (i + 1) * half] + got.astype(F32)

    begin = lax.optimization_barrier((keep, *[local(keep, i).astype(BF16) for i in range(3)]))
    far_sum = onward(begin[1], 2)
    third = onward(begin[2], 1)
    third_twin = onward(begin[3], 1)
    ones = lax.optimization_barrier((begin[0], local(begin[0], 3).astype(BF16), local(begin[0], 4).astype(BF16)))
    by_one = onward(ones[1], 1)
    by_one_twin = onward(ones[2], 1, 1, 1)
    twos = lax.optimization_barrier((ones[0], (local(ones[0], 6) + third_twin.astype(F32)).astype(BF16)))
    by_two_twin = onward(twos[1], 2, 1, 1)
    by_two = onward((local(twos[0], 5) + far_sum.astype(F32) + third.astype(F32)).astype(BF16), 2)
    hamiltonian = pl.pallas_call(
        finish_kernel,
        in_specs=[vmem] * 6,
        out_specs=vmem,
        out_shape=jax.ShapeDtypeStruct(density_blocks.shape, F32),
        compiler_params=params,
        name="finish",
    )(keep, got_rest, by_one, by_two, by_one_twin, by_two_twin)
    return potential.reshape(cells_x, cells_z, line_cells), hamiltonian


def solution(mesh):
    placed = (
        P("col", "height", None, None),
        P("col", "height"),
        P("col", "height", None, None),
        P(("col", "height"), None, None),
    )
    return jax.shard_map(
        per_device,
        mesh=mesh,
        in_specs=placed,
        out_specs=(P("col", "height", None), P(("col", "height"), None, None)),
        check_vma=False,
    )
```

```python
import functools

import jax
import jax.numpy as jnp
import numpy as np
from jax import lax
from jax.experimental import pallas as pl
from jax.experimental.pallas import tpu as pltpu
from jax.sharding import PartitionSpec as P

XC_COEF = 0.7386
FOUR_PI = 12.566370614359172
KAPPA = 0.5
LANES = 128
F32 = jnp.float32
BF16 = jnp.bfloat16
HIGHEST = lax.Precision.HIGHEST
VMEM_LIMIT = 12 * 1024 * 1024
STAGE_LIMIT = 44 * 1024 * 1024
SUMS_LIMIT = 24 * 1024 * 1024
LINES_AT_ONCE = 8


def cas_table(count):
    steps = np.arange(count)
    angle = 2.0 * np.pi * (steps[:, None] * steps[None, :] % count) / count
    return (np.cos(angle) + np.sin(angle)).astype(np.float32)


def symbol(count):
    return (2.0 - 2.0 * np.cos(2.0 * np.pi * np.arange(count) / count)).astype(np.float32)


def block_base(height, chips, share, place):
    distance, flip = place
    core = lax.rem(height, 2)
    chip = lax.rem(height // 2 + distance * (1 - 2 * core) + chips, chips)
    return (chip * 2 + (1 - core if flip else core)) * share


def masked_line(orb_ref, line, live):
    parts = []
    for a in range(4):
        rows = orb_ref[line, a * 64 : (a + 1) * 64, :]
        parts.append(rows if a == 0 else jnp.where(a < live, rows, jnp.zeros((), BF16)))
    return jnp.concatenate(parts, axis=0)


def stage_kernel(live_ref, orb_hbm, orb_ref, order_ref, count_ref, sem):
    copy = pltpu.make_async_copy(orb_hbm, orb_ref, sem)
    copy.start()
    lines = orb_ref.shape[0]
    for n in range(4):
        count_ref[n] = 0

    def place(line, carry):
        n = live_ref[line] - 1
        order_ref[n, count_ref[n]] = line
        count_ref[n] += 1
        return carry

    lax.fori_loop(0, lines, place, 0)
    for n in range(4):
        for i in range(LINES_AT_ONCE):
            order_ref[n, count_ref[n] + i] = lines
    copy.wait()


def density_kernel(index_ref, live_ref, part_ref, orb_ref, *refs, chunk, places, chips):
    pieces, (cas_ref, dens_ref, spec_ref, table_ref) = refs[:-4], refs[-4:]
    packed_rows = table_ref.shape[0] // 2

    at = 0
    for piece in pieces:
        for first in range(0, piece.shape[0], 8):
            base = block_base(part_ref[2], chips, 8, places[at])
            at += 1
            both = piece[first : first + 8]
            table_ref[pl.ds(base, 8)] = both
            table_ref[pl.ds(packed_rows + base, 8)] = pltpu.roll(both, 64, 2)
    left_lanes = lax.broadcasted_iota(jnp.int32, (64, LANES), 1) < 64

    def body(i, carry):
        first = i * chunk
        rows_out = []
        for l in range(chunk):
            line = first + l
            phi = masked_line(orb_ref, line, live_ref[line])
            strips = []
            for a in range(4):
                halves = []
                for b in (0, 2):
                    at = line * 16 + a * 4 + b
                    halves.append(jnp.where(left_lanes, table_ref[index_ref[at]], table_ref[index_ref[at + 1]]))
                strips.append(jnp.concatenate(halves, axis=1))
            matrix = jnp.concatenate(strips, axis=0)
            product = jnp.dot(matrix, phi, preferred_element_type=F32)
            rows_out.append(jnp.sum(phi.astype(F32) * product, axis=0, keepdims=True))
        dens_ref[pl.ds(pl.multiple_of(first, 8), chunk), :] = jnp.concatenate(rows_out, axis=0)
        return carry

    lax.fori_loop(0, orb_ref.shape[0] // chunk, body, 0)
    spectrum = jnp.dot(dens_ref[...], cas_ref[...], precision=HIGHEST, preferred_element_type=F32)
    lines = spectrum.shape[0]
    wide = jnp.concatenate([spectrum, jnp.zeros((LANES - lines, spectrum.shape[1]), F32)], axis=0)
    spec_ref[...] = wide.T


def solve_kernel(part_ref, in_ref, cx_ref, cxt_ref, cz_ref, sx_ref, sz_ref, sy_ref, out_ref, *, cells_x, cells_z, cols, heights):
    core = part_ref[0]
    plane = part_ref[1]
    lane = lax.broadcasted_iota(jnp.int32, (cols, LANES), 1)
    group_of = lane // cells_z
    slots = LANES // cells_z
    skewed = [
        pltpu.roll(in_ref[pl.ds(h, cols, stride=heights), :], cells_z * h, 1) if h else in_ref[pl.ds(h, cols, stride=heights), :]
        for h in range(heights)
    ]
    rows = []
    for x in range(cells_x):
        mixed = jnp.zeros((cols, LANES), F32)
        for g in range(slots):
            mixed = jnp.where(group_of == g, skewed[(g - x) % slots], mixed)
        rows.append(pltpu.roll(mixed, LANES - cells_z * x, 1) if x else mixed)
    field = jnp.concatenate(rows, axis=0)
    forward = cx_ref[core]
    spec = jnp.dot(forward, field, precision=HIGHEST, preferred_element_type=F32)
    spec = jnp.dot(spec, cz_ref[...], precision=HIGHEST, preferred_element_type=F32)
    scale = sx_ref[core] + sz_ref[...] + sy_ref[plane]
    spec = spec / scale
    spec = jnp.dot(spec, cz_ref[...], precision=HIGHEST, preferred_element_type=F32)
    back = jnp.dot(cxt_ref[core], spec, precision=HIGHEST, preferred_element_type=F32)
    skewed = []
    for x in range(cells_x):
        part = back[x * cols : (x + 1) * cols]
        skewed.append(pltpu.roll(part, cells_z * x, 1) if x else part)
    for h in range(heights):
        mixed = jnp.zeros((cols, LANES), F32)
        for x in range(cells_x):
            mixed = jnp.where(group_of == (h + x) % slots, skewed[x], mixed)
        mixed = pltpu.roll(mixed, LANES - cells_z * h, 1) if h else mixed
        out_ref[pl.ds(h, cols, stride=heights), :] = mixed


def hamiltonian_kernel(
    pair_ref,
    order_ref,
    count_ref,
    part_ref,
    orb_ref,
    dens_ref,
    back_ref,
    cas_ref,
    pot_ref,
    keep_ref,
    first_ref,
    rest_ref,
    left_ref,
    right_ref,
    padded_ref,
    *,
    places,
    chips,
):
    lines = dens_ref.shape[0]

    def clear(i, carry):
        left_ref[pl.ds(i * 8, 8)] = jnp.zeros((8, 64, LANES), F32)
        right_ref[pl.ds(i * 8, 8)] = jnp.zeros((8, 64, LANES), F32)
        return carry

    lax.fori_loop(0, left_ref.shape[0] // 8, clear, 0)
    hartree = jnp.dot(cas_ref[...], back_ref[...], precision=HIGHEST, preferred_element_type=F32).T
    dens = dens_ref[...]
    potential = hartree[:lines] - XC_COEF * jnp.exp(jnp.log(dens * dens + 1.0) * (1.0 / 6.0))
    pot_ref[...] = potential
    padded_ref[...] = jnp.concatenate([potential, jnp.zeros((padded_ref.shape[0] - lines, LANES), F32)], axis=0)

    for n in range(1, 5):

        def body(i, carry, n=n):
            for j in range(LINES_AT_ONCE):
                entry = order_ref[n - 1, i * LINES_AT_ONCE + j]
                line = jnp.minimum(entry, lines - 1)
                rows = orb_ref[line, : n * 64, :]
                phi = rows if n % 2 == 0 else jnp.concatenate([rows, jnp.zeros((64, LANES), BF16)], axis=0)
                weighted = (rows.astype(F32) * padded_ref[pl.ds(entry, 1), :]).astype(BF16)
                full = lax.dot_general(weighted, phi, (((1,), (1,)), ((), ())), preferred_element_type=F32)
                for a in range(n):
                    for b in range(0, n, 2):
                        at = line * 16 + a * 4 + b
                        both = full[a * 64 : (a + 1) * 64, b * 64 : b * 64 + LANES]
                        left_ref[pair_ref[at]] += both
                        if b + 1 < n:
                            right_ref[pair_ref[at + 1]] += both
            return carry

        lax.fori_loop(0, (count_ref[n - 1] + LINES_AT_ONCE - 1) // LINES_AT_ONCE, body, 0)
    left_lanes = lax.broadcasted_iota(jnp.int32, (8, 64, LANES), 2) < 64

    def emit(base):
        low, high = pl.ds(base, 8), pl.ds(base + 8, 8)
        crossed = jnp.where(left_lanes, left_ref[high], right_ref[low])
        return jnp.where(left_lanes, left_ref[low], right_ref[high]) + pltpu.roll(crossed, 64, 2)

    at = 0
    for out in (keep_ref, first_ref, rest_ref):
        for first in range(0, out.shape[0], 8):
            out[first : first + 8] = emit(block_base(part_ref[2], chips, 16, places[at])).astype(out.dtype)
            at += 1


def finish_kernel(keep_ref, got_ref, one_ref, two_ref, twin_one_ref, twin_two_ref, out_ref):
    rows = out_ref.shape[0] // 2
    for i in range(rows):
        total = keep_ref[keep_ref.shape[0] - rows + i] + got_ref[got_ref.shape[0] - rows + i].astype(F32)
        total = total + one_ref[i].astype(F32) + two_ref[i].astype(F32)
        total = total + twin_one_ref[i].astype(F32) + twin_two_ref[i].astype(F32)
        out_ref[i] = total[:, :64]
        out_ref[rows + i] = total[:, 64:]


def per_device(orbitals, live_atoms, pair_index, density_blocks):
    cells_x, cells_z, width, line_cells = orbitals.shape
    cols = lax.axis_size("col")
    heights = lax.axis_size("height")
    full_x = cells_x * cols
    full_z = cells_z * heights
    lines = cells_x * cells_z
    share = density_blocks.shape[0]
    devices = cols * heights
    copies = devices // line_cells
    chunk = 16
    block_rows = share * heights // 2

    cas_y = cas_table(line_cells)
    cas_y2 = np.repeat(cas_y, copies, axis=1)
    cas_x = cas_table(full_x)
    order = np.arange(full_x).reshape(cols, cells_x).T.reshape(-1)
    half_x = full_x // copies
    forward_x = cas_x.reshape(copies, half_x, full_x)[:, :, order]
    back_x = forward_x.transpose(0, 2, 1).copy()
    cas_z = cas_table(full_z)
    norm = 1.0 / (full_x * full_z * line_cells)
    unit = FOUR_PI * norm
    sym_x = np.broadcast_to(symbol(full_x).reshape(copies, half_x, 1) / unit, (copies, half_x, LANES)).astype(np.float32)
    sym_z = ((symbol(full_z) + KAPPA * KAPPA) / unit).reshape(1, full_z).astype(np.float32)
    sym_y = (symbol(line_cells) / unit).astype(np.float32)

    orb = orbitals.reshape(lines, width, line_cells)
    live = live_atoms.reshape(lines)
    pairs = pair_index.reshape(lines * 16)
    packed = jnp.concatenate([density_blocks[: share // 2], density_blocks[share // 2 :]], axis=2)
    chips = heights // 2
    far = chips // 2
    height = lax.axis_index("height")
    device = lax.axis_index("col") * heights + height
    part = jnp.stack([device % copies, device // copies, height]).astype(jnp.int32)
    twin = [(h, h ^ 1) for h in range(heights)]

    def across(values):
        return lax.ppermute(values, "height", twin)

    def onward(values, hops, sign=1, flip=0):
        def target(h):
            core = h % 2
            return (h // 2 + sign * hops * (1 - 2 * core)) % chips * 2 + (core ^ flip)

        return lax.ppermute(values, "height", [(h, target(h)) for h in range(heights)])

    half = share // 2
    gather_places = [(0, 0), (0, 1)]
    gather_places += [(-2, 0), (2, 1), (-2, 1), (2, 0), (-1, 0), (-1, 1), (1, 1), (1, 0)]
    gather_places += [(-3, 0), (3, 1), (-3, 1), (3, 0)]
    gather_places += [(far, 0), (far, 1)]
    keep_places, give_places = [(far, 0)], [(far, 1)]
    for d in (3, 1, 2):
        keep_places += [(d, 0), (d, 1)]
        give_places += [(-d, 1), (-d, 0)]
    sum_places = keep_places + [(0, 0)] + give_places + [(0, 1)]

    side = jnp.arange(lines * 16, dtype=jnp.int32) % 2
    table_index = (pairs // share) * half + pairs % half
    table_index = table_index + jnp.where((pairs // half) % 2 == side, 0, block_rows)
    twin_packed = across(packed)
    second = onward(packed, 2)
    second_twin = onward(twin_packed, 2)
    whole_chip = jnp.concatenate([packed, twin_packed], axis=0)
    near = onward(whole_chip, 1)
    smem = pl.BlockSpec(memory_space=pltpu.SMEM)
    vmem = pl.BlockSpec(memory_space=pltpu.VMEM)
    params = pltpu.CompilerParams(vmem_limit_bytes=VMEM_LIMIT)
    orb, order, count = pl.pallas_call(
        stage_kernel,
        in_specs=[smem, pl.BlockSpec(memory_space=pl.ANY)],
        out_specs=[vmem, smem, smem],
        out_shape=[
            jax.ShapeDtypeStruct(orb.shape, BF16),
            jax.ShapeDtypeStruct((4, lines + LINES_AT_ONCE), jnp.int32),
            jax.ShapeDtypeStruct((4,), jnp.int32),
        ],
        scratch_shapes=[pltpu.SemaphoreType.DMA(())],
        compiler_params=pltpu.CompilerParams(vmem_limit_bytes=STAGE_LIMIT),
        name="stage",
    )(live, orb)
    second_twin, near, table_index, live, part, pairs, orb, order, count = lax.optimization_barrier(
        (second_twin, near, table_index, live, part, pairs, orb, order, count)
    )
    fourth = onward(second, 2)
    rest = [onward(second, 1), onward(second_twin, 1)]
    pieces = [whole_chip]
    for piece in (second, second_twin, near, *rest, fourth):
        pieces += [piece, across(piece)]
    density, spectrum = pl.pallas_call(
        functools.partial(density_kernel, chunk=chunk, places=gather_places, chips=chips),
        in_specs=[smem] * 3 + [vmem] * (len(pieces) + 2),
        out_specs=[vmem, vmem],
        out_shape=[
            jax.ShapeDtypeStruct((lines, line_cells), F32),
            jax.ShapeDtypeStruct((devices, LANES), F32),
        ],
        scratch_shapes=[pltpu.VMEM((2 * block_rows, 64, LANES), BF16)],
        compiler_params=params,
        name="density",
    )(table_index, live, part, orb, *pieces, jnp.asarray(cas_y2))

    def exchange(values):
        out = lax.all_to_all(values.reshape(devices, 1, LANES), ("col", "height"), split_axis=0, concat_axis=0, tiled=True)
        return out.reshape(devices, LANES)

    solved = pl.pallas_call(
        lambda *refs: solve_kernel(*refs, cells_x=cells_x, cells_z=cells_z, cols=cols, heights=heights),
        in_specs=[smem, vmem, vmem, vmem, vmem, vmem, vmem, smem],
        out_specs=vmem,
        out_shape=jax.ShapeDtypeStruct((devices, LANES), F32),
        compiler_params=params,
        name="solve",
    )(
        part,
        exchange(spectrum),
        jnp.asarray(forward_x),
        jnp.asarray(back_x),
        jnp.asarray(cas_z),
        jnp.asarray(sym_x),
        jnp.asarray(sym_z),
        jnp.asarray(sym_y),
    )
    returned = exchange(solved)

    half_rows = block_rows // 2
    potential, keep, give_first, give_rest = pl.pallas_call(
        functools.partial(hamiltonian_kernel, places=sum_places, chips=chips),
        in_specs=[smem] * 4 + [vmem] * 4,
        out_specs=[vmem] * 4,
        out_shape=[
            jax.ShapeDtypeStruct((lines, line_cells), F32),
            jax.ShapeDtypeStruct((half_rows, 64, LANES), F32),
            jax.ShapeDtypeStruct((3 * share // 2, 64, LANES), BF16),
            jax.ShapeDtypeStruct((half_rows - 3 * share // 2, 64, LANES), BF16),
        ],
        scratch_shapes=[
            pltpu.VMEM((2 * block_rows, 64, LANES), F32),
            pltpu.VMEM((2 * block_rows, 64, LANES), F32),
            pltpu.VMEM((lines + 8, LANES), F32),
        ],
        compiler_params=pltpu.CompilerParams(vmem_limit_bytes=SUMS_LIMIT),
        name="hamiltonian",
    )(pairs, order, count, part, orb, density, returned, jnp.asarray(cas_y2))

    got_first = across(give_first)
    got_rest = across(lax.optimization_barrier((give_rest, got_first))[0])

    def local(kept, i):
        got = got_first[i * half : (i + 1) * half] if i < 3 else got_rest[(i - 3) * half : (i - 2) * half]
        return kept[i * half : (i + 1) * half] + got.astype(F32)

    begin = lax.optimization_barrier((keep, *[local(keep, i).astype(BF16) for i in range(3)]))
    far_sum = onward(begin[1], 2)
    third = onward(begin[2], 1)
    third_twin = onward(begin[3], 1)
    ones = lax.optimization_barrier((begin[0], local(begin[0], 3).astype(BF16), local(begin[0], 4).astype(BF16)))
    by_one = onward(ones[1], 1)
    by_one_twin = onward(ones[2], 1, 1, 1)
    twos = lax.optimization_barrier((ones[0], (local(ones[0], 6) + third_twin.astype(F32)).astype(BF16)))
    by_two_twin = onward(twos[1], 2, 1, 1)
    by_two = onward((local(twos[0], 5) + far_sum.astype(F32) + third.astype(F32)).astype(BF16), 2)
    hamiltonian = pl.pallas_call(
        finish_kernel,
        in_specs=[vmem] * 6,
        out_specs=vmem,
        out_shape=jax.ShapeDtypeStruct(density_blocks.shape, F32),
        compiler_params=params,
        name="finish",
    )(keep, got_rest, by_one, by_two, by_one_twin, by_two_twin)
    return potential.reshape(cells_x, cells_z, line_cells), hamiltonian


def solution(mesh):
    placed = (
        P("col", "height", None, None),
        P("col", "height"),
        P("col", "height", None, None),
        P(("col", "height"), None, None),
    )
    return jax.shard_map(
        per_device,
        mesh=mesh,
        in_specs=placed,
        out_specs=(P("col", "height", None), P(("col", "height"), None, None)),
        check_vma=False,
    )
```

```python
import functools

import jax
import jax.numpy as jnp
import numpy as np
from jax import lax
from jax.experimental import pallas as pl
from jax.experimental.pallas import tpu as pltpu
from jax.sharding import PartitionSpec as P

XC_COEF = 0.7386
FOUR_PI = 12.566370614359172
KAPPA = 0.5
LANES = 128
F32 = jnp.float32
BF16 = jnp.bfloat16
HIGHEST = lax.Precision.HIGHEST
VMEM_LIMIT = 12 * 1024 * 1024
STAGE_LIMIT = 44 * 1024 * 1024
SUMS_LIMIT = 24 * 1024 * 1024
LINES_AT_ONCE = 8


def cas_table(count):
    steps = np.arange(count)
    angle = 2.0 * np.pi * (steps[:, None] * steps[None, :] % count) / count
    return (np.cos(angle) + np.sin(angle)).astype(np.float32)


def symbol(count):
    return (2.0 - 2.0 * np.cos(2.0 * np.pi * np.arange(count) / count)).astype(np.float32)


def block_base(height, chips, share, place):
    distance, flip = place
    core = lax.rem(height, 2)
    chip = lax.rem(height // 2 + distance * (1 - 2 * core) + chips, chips)
    return (chip * 2 + (1 - core if flip else core)) * share


def masked_line(orb_ref, line, live):
    parts = []
    for a in range(4):
        rows = orb_ref[line, a * 64 : (a + 1) * 64, :]
        parts.append(rows if a == 0 else jnp.where(a < live, rows, jnp.zeros((), BF16)))
    return jnp.concatenate(parts, axis=0)


def stage_kernel(live_ref, orb_hbm, orb_ref, order_ref, count_ref, sem):
    copy = pltpu.make_async_copy(orb_hbm, orb_ref, sem)
    copy.start()
    lines = orb_ref.shape[0]
    for n in range(4):
        count_ref[n] = 0

    def place(line, carry):
        n = live_ref[line] - 1
        order_ref[n, count_ref[n]] = line
        count_ref[n] += 1
        return carry

    lax.fori_loop(0, lines, place, 0)
    for n in range(4):
        for i in range(LINES_AT_ONCE):
            order_ref[n, count_ref[n] + i] = lines
    copy.wait()


def density_kernel(index_ref, live_ref, part_ref, orb_ref, *refs, chunk, places, chips):
    pieces, (cas_ref, dens_ref, spec_ref, table_ref) = refs[:-4], refs[-4:]
    packed_rows = table_ref.shape[0] // 2

    at = 0
    for piece in pieces:
        for first in range(0, piece.shape[0], 8):
            base = block_base(part_ref[2], chips, 8, places[at])
            at += 1
            both = piece[first : first + 8]
            table_ref[pl.ds(base, 8)] = both
            table_ref[pl.ds(packed_rows + base, 8)] = pltpu.roll(both, 64, 2)
    left_lanes = lax.broadcasted_iota(jnp.int32, (64, LANES), 1) < 64

    def body(i, carry):
        first = i * chunk
        rows_out = []
        for l in range(chunk):
            line = first + l
            phi = masked_line(orb_ref, line, live_ref[line])
            strips = []
            for a in range(4):
                halves = []
                for b in (0, 2):
                    at = line * 16 + a * 4 + b
                    halves.append(jnp.where(left_lanes, table_ref[index_ref[at]], table_ref[index_ref[at + 1]]))
                strips.append(jnp.concatenate(halves, axis=1))
            matrix = jnp.concatenate(strips, axis=0)
            product = jnp.dot(matrix, phi, preferred_element_type=F32)
            rows_out.append(jnp.sum(phi.astype(F32) * product, axis=0, keepdims=True))
        dens_ref[pl.ds(pl.multiple_of(first, 8), chunk), :] = jnp.concatenate(rows_out, axis=0)
        return carry

    lax.fori_loop(0, orb_ref.shape[0] // chunk, body, 0)
    spectrum = jnp.dot(dens_ref[...], cas_ref[...], precision=HIGHEST, preferred_element_type=F32)
    lines = spectrum.shape[0]
    wide = jnp.concatenate([spectrum, jnp.zeros((LANES - lines, spectrum.shape[1]), F32)], axis=0)
    spec_ref[...] = wide.T


def solve_kernel(part_ref, in_ref, cx_ref, cxt_ref, cz_ref, sx_ref, sz_ref, sy_ref, out_ref, *, cells_x, cells_z, cols, heights):
    core = part_ref[0]
    plane = part_ref[1]
    lane = lax.broadcasted_iota(jnp.int32, (cols, LANES), 1)
    group_of = lane // cells_z
    slots = LANES // cells_z
    skewed = [
        pltpu.roll(in_ref[pl.ds(h, cols, stride=heights), :], cells_z * h, 1) if h else in_ref[pl.ds(h, cols, stride=heights), :]
        for h in range(heights)
    ]
    rows = []
    for x in range(cells_x):
        mixed = jnp.zeros((cols, LANES), F32)
        for g in range(slots):
            mixed = jnp.where(group_of == g, skewed[(g - x) % slots], mixed)
        rows.append(pltpu.roll(mixed, LANES - cells_z * x, 1) if x else mixed)
    field = jnp.concatenate(rows, axis=0)
    forward = cx_ref[core]
    spec = jnp.dot(forward, field, precision=HIGHEST, preferred_element_type=F32)
    spec = jnp.dot(spec, cz_ref[...], precision=HIGHEST, preferred_element_type=F32)
    scale = sx_ref[core] + sz_ref[...] + sy_ref[plane]
    spec = spec / scale
    spec = jnp.dot(spec, cz_ref[...], precision=HIGHEST, preferred_element_type=F32)
    back = jnp.dot(cxt_ref[core], spec, precision=HIGHEST, preferred_element_type=F32)
    skewed = []
    for x in range(cells_x):
        part = back[x * cols : (x + 1) * cols]
        skewed.append(pltpu.roll(part, cells_z * x, 1) if x else part)
    for h in range(heights):
        mixed = jnp.zeros((cols, LANES), F32)
        for x in range(cells_x):
            mixed = jnp.where(group_of == (h + x) % slots, skewed[x], mixed)
        mixed = pltpu.roll(mixed, LANES - cells_z * h, 1) if h else mixed
        out_ref[pl.ds(h, cols, stride=heights), :] = mixed


def hamiltonian_kernel(
    pair_ref,
    order_ref,
    count_ref,
    part_ref,
    orb_ref,
    dens_ref,
    back_ref,
    cas_ref,
    pot_ref,
    keep_ref,
    first_ref,
    rest_ref,
    left_ref,
    right_ref,
    padded_ref,
    *,
    places,
    chips,
):
    lines = dens_ref.shape[0]

    def clear(i, carry):
        left_ref[pl.ds(i * 8, 8)] = jnp.zeros((8, 64, LANES), F32)
        right_ref[pl.ds(i * 8, 8)] = jnp.zeros((8, 64, LANES), F32)
        return carry

    lax.fori_loop(0, left_ref.shape[0] // 8, clear, 0)
    hartree = jnp.dot(cas_ref[...], back_ref[...], precision=HIGHEST, preferred_element_type=F32).T
    dens = dens_ref[...]
    potential = hartree[:lines] - XC_COEF * jnp.exp(jnp.log(dens * dens + 1.0) * (1.0 / 6.0))
    pot_ref[...] = potential
    padded_ref[...] = jnp.concatenate([potential, jnp.zeros((padded_ref.shape[0] - lines, LANES), F32)], axis=0)

    for n in range(1, 5):

        def body(i, carry, n=n):
            for j in range(LINES_AT_ONCE):
                entry = order_ref[n - 1, i * LINES_AT_ONCE + j]
                line = jnp.minimum(entry, lines - 1)
                rows = orb_ref[line, : n * 64, :]
                phi = rows if n % 2 == 0 else jnp.concatenate([rows, jnp.zeros((64, LANES), BF16)], axis=0)
                weighted = (rows.astype(F32) * padded_ref[pl.ds(entry, 1), :]).astype(BF16)
                full = lax.dot_general(weighted, phi, (((1,), (1,)), ((), ())), preferred_element_type=F32)
                for a in range(n):
                    for b in range(0, n, 2):
                        at = line * 16 + a * 4 + b
                        both = full[a * 64 : (a + 1) * 64, b * 64 : b * 64 + LANES]
                        left_ref[pair_ref[at]] += both
                        if b + 1 < n:
                            right_ref[pair_ref[at + 1]] += both
            return carry

        lax.fori_loop(0, (count_ref[n - 1] + LINES_AT_ONCE - 1) // LINES_AT_ONCE, body, 0)
    left_lanes = lax.broadcasted_iota(jnp.int32, (8, 64, LANES), 2) < 64

    def emit(base):
        low, high = pl.ds(base, 8), pl.ds(base + 8, 8)
        crossed = jnp.where(left_lanes, left_ref[high], right_ref[low])
        return jnp.where(left_lanes, left_ref[low], right_ref[high]) + pltpu.roll(crossed, 64, 2)

    at = 0
    for out in (keep_ref, first_ref, rest_ref):
        for first in range(0, out.shape[0], 8):
            out[first : first + 8] = emit(block_base(part_ref[2], chips, 16, places[at])).astype(out.dtype)
            at += 1


def finish_kernel(keep_ref, got_ref, one_ref, two_ref, twin_one_ref, twin_two_ref, out_ref):
    rows = out_ref.shape[0] // 2
    for i in range(rows):
        total = keep_ref[keep_ref.shape[0] - rows + i] + got_ref[got_ref.shape[0] - rows + i].astype(F32)
        total = total + one_ref[rows + i].astype(F32) + two_ref[i].astype(F32)
        total = total + twin_one_ref[i].astype(F32) + twin_two_ref[i].astype(F32)
        out_ref[i] = total[:, :64]
        out_ref[rows + i] = total[:, 64:]


def per_device(orbitals, live_atoms, pair_index, density_blocks):
    cells_x, cells_z, width, line_cells = orbitals.shape
    cols = lax.axis_size("col")
    heights = lax.axis_size("height")
    full_x = cells_x * cols
    full_z = cells_z * heights
    lines = cells_x * cells_z
    share = density_blocks.shape[0]
    devices = cols * heights
    copies = devices // line_cells
    chunk = 16
    block_rows = share * heights // 2

    cas_y = cas_table(line_cells)
    cas_y2 = np.repeat(cas_y, copies, axis=1)
    cas_x = cas_table(full_x)
    order = np.arange(full_x).reshape(cols, cells_x).T.reshape(-1)
    half_x = full_x // copies
    forward_x = cas_x.reshape(copies, half_x, full_x)[:, :, order]
    back_x = forward_x.transpose(0, 2, 1).copy()
    cas_z = cas_table(full_z)
    norm = 1.0 / (full_x * full_z * line_cells)
    unit = FOUR_PI * norm
    sym_x = np.broadcast_to(symbol(full_x).reshape(copies, half_x, 1) / unit, (copies, half_x, LANES)).astype(np.float32)
    sym_z = ((symbol(full_z) + KAPPA * KAPPA) / unit).reshape(1, full_z).astype(np.float32)
    sym_y = (symbol(line_cells) / unit).astype(np.float32)

    orb = orbitals.reshape(lines, width, line_cells)
    live = live_atoms.reshape(lines)
    pairs = pair_index.reshape(lines * 16)
    packed = jnp.concatenate([density_blocks[: share // 2], density_blocks[share // 2 :]], axis=2)
    chips = heights // 2
    far = chips // 2
    height = lax.axis_index("height")
    device = lax.axis_index("col") * heights + height
    part = jnp.stack([device % copies, device // copies, height]).astype(jnp.int32)
    twin = [(h, h ^ 1) for h in range(heights)]

    def across(values):
        return lax.ppermute(values, "height", twin)

    def onward(values, hops, sign=1, flip=0):
        def target(h):
            core = h % 2
            return (h // 2 + sign * hops * (1 - 2 * core)) % chips * 2 + (core ^ flip)

        return lax.ppermute(values, "height", [(h, target(h)) for h in range(heights)])

    half = share // 2
    gather_places = [(0, 0), (0, 1)]
    gather_places += [(-2, 0), (2, 1), (-2, 1), (2, 0), (-1, 0), (-1, 1), (1, 1), (1, 0)]
    gather_places += [(-3, 0), (3, 1), (-3, 1), (3, 0)]
    gather_places += [(far, 0), (far, 1)]
    keep_places = [(far, 0), (3, 0), (1, 0), (3, 1), (1, 1), (2, 0), (2, 1), (0, 0)]
    sum_places = keep_places + [(-d, 1 - flip) for d, flip in keep_places]

    side = jnp.arange(lines * 16, dtype=jnp.int32) % 2
    table_index = (pairs // share) * half + pairs % half
    table_index = table_index + jnp.where((pairs // half) % 2 == side, 0, block_rows)
    twin_packed = across(packed)
    second = onward(packed, 2)
    second_twin = onward(twin_packed, 2)
    whole_chip = jnp.concatenate([packed, twin_packed], axis=0)
    near = onward(whole_chip, 1)
    smem = pl.BlockSpec(memory_space=pltpu.SMEM)
    vmem = pl.BlockSpec(memory_space=pltpu.VMEM)
    params = pltpu.CompilerParams(vmem_limit_bytes=VMEM_LIMIT)
    orb, order, count = pl.pallas_call(
        stage_kernel,
        in_specs=[smem, pl.BlockSpec(memory_space=pl.ANY)],
        out_specs=[vmem, smem, smem],
        out_shape=[
            jax.ShapeDtypeStruct(orb.shape, BF16),
            jax.ShapeDtypeStruct((4, lines + LINES_AT_ONCE), jnp.int32),
            jax.ShapeDtypeStruct((4,), jnp.int32),
        ],
        scratch_shapes=[pltpu.SemaphoreType.DMA(())],
        compiler_params=pltpu.CompilerParams(vmem_limit_bytes=STAGE_LIMIT),
        name="stage",
    )(live, orb)
    second_twin, near, table_index, live, part, pairs, orb, order, count = lax.optimization_barrier(
        (second_twin, near, table_index, live, part, pairs, orb, order, count)
    )
    fourth = onward(second, 2)
    rest = [onward(second, 1), onward(second_twin, 1)]
    pieces = [whole_chip]
    for piece in (second, second_twin, near, *rest, fourth):
        pieces += [piece, across(piece)]
    density, spectrum = pl.pallas_call(
        functools.partial(density_kernel, chunk=chunk, places=gather_places, chips=chips),
        in_specs=[smem] * 3 + [vmem] * (len(pieces) + 2),
        out_specs=[vmem, vmem],
        out_shape=[
            jax.ShapeDtypeStruct((lines, line_cells), F32),
            jax.ShapeDtypeStruct((devices, LANES), F32),
        ],
        scratch_shapes=[pltpu.VMEM((2 * block_rows, 64, LANES), BF16)],
        compiler_params=params,
        name="density",
    )(table_index, live, part, orb, *pieces, jnp.asarray(cas_y2))

    def exchange(values):
        out = lax.all_to_all(values.reshape(devices, 1, LANES), ("col", "height"), split_axis=0, concat_axis=0, tiled=True)
        return out.reshape(devices, LANES)

    solved = pl.pallas_call(
        lambda *refs: solve_kernel(*refs, cells_x=cells_x, cells_z=cells_z, cols=cols, heights=heights),
        in_specs=[smem, vmem, vmem, vmem, vmem, vmem, vmem, smem],
        out_specs=vmem,
        out_shape=jax.ShapeDtypeStruct((devices, LANES), F32),
        compiler_params=params,
        name="solve",
    )(
        part,
        exchange(spectrum),
        jnp.asarray(forward_x),
        jnp.asarray(back_x),
        jnp.asarray(cas_z),
        jnp.asarray(sym_x),
        jnp.asarray(sym_z),
        jnp.asarray(sym_y),
    )
    returned = exchange(solved)

    half_rows = block_rows // 2
    potential, keep, give_first, give_rest = pl.pallas_call(
        functools.partial(hamiltonian_kernel, places=sum_places, chips=chips),
        in_specs=[smem] * 4 + [vmem] * 4,
        out_specs=[vmem] * 4,
        out_shape=[
            jax.ShapeDtypeStruct((lines, line_cells), F32),
            jax.ShapeDtypeStruct((half_rows, 64, LANES), F32),
            jax.ShapeDtypeStruct((2 * share, 64, LANES), BF16),
            jax.ShapeDtypeStruct((half_rows - 2 * share, 64, LANES), BF16),
        ],
        scratch_shapes=[
            pltpu.VMEM((2 * block_rows, 64, LANES), F32),
            pltpu.VMEM((2 * block_rows, 64, LANES), F32),
            pltpu.VMEM((lines + 8, LANES), F32),
        ],
        compiler_params=pltpu.CompilerParams(vmem_limit_bytes=SUMS_LIMIT),
        name="hamiltonian",
    )(pairs, order, count, part, orb, density, returned, jnp.asarray(cas_y2))

    got_first = across(give_first)
    got_rest = across(lax.optimization_barrier((give_rest, got_first))[0])

    def local(kept, i, count=1):
        got = got_first[i * half : (i + count) * half] if i < 4 else got_rest[(i - 4) * half : (i - 4 + count) * half]
        return kept[i * half : (i + count) * half] + got.astype(F32)

    begin = lax.optimization_barrier(
        (keep, local(keep, 0).astype(BF16), local(keep, 1, 2).astype(BF16), local(keep, 3).astype(BF16))
    )
    far_sum = onward(begin[1], 2)
    ahead = onward(begin[2], 1)
    third_twin = onward(begin[3], 1)
    ones = lax.optimization_barrier((begin[0], local(begin[0], 4).astype(BF16)))
    by_one_twin = onward(ones[1], 1, 1, 1)
    twos = lax.optimization_barrier((ones[0], (local(ones[0], 6) + third_twin.astype(F32)).astype(BF16)))
    by_two_twin = onward(twos[1], 2, 1, 1)
    by_two = onward((local(twos[0], 5) + far_sum.astype(F32) + ahead[:half].astype(F32)).astype(BF16), 2)
    hamiltonian = pl.pallas_call(
        finish_kernel,
        in_specs=[vmem] * 6,
        out_specs=vmem,
        out_shape=jax.ShapeDtypeStruct(density_blocks.shape, F32),
        compiler_params=params,
        name="finish",
    )(keep, got_rest, ahead, by_two, by_one_twin, by_two_twin)
    return potential.reshape(cells_x, cells_z, line_cells), hamiltonian


def solution(mesh):
    placed = (
        P("col", "height", None, None),
        P("col", "height"),
        P("col", "height", None, None),
        P(("col", "height"), None, None),
    )
    return jax.shard_map(
        per_device,
        mesh=mesh,
        in_specs=placed,
        out_specs=(P("col", "height", None), P(("col", "height"), None, None)),
        check_vma=False,
    )
```

```python
import functools

import jax
import jax.numpy as jnp
import numpy as np
from jax import lax
from jax.experimental import pallas as pl
from jax.experimental.pallas import tpu as pltpu
from jax.sharding import PartitionSpec as P

XC_COEF = 0.7386
FOUR_PI = 12.566370614359172
KAPPA = 0.5
LANES = 128
F32 = jnp.float32
BF16 = jnp.bfloat16
HIGHEST = lax.Precision.HIGHEST
VMEM_LIMIT = 12 * 1024 * 1024
STAGE_LIMIT = 44 * 1024 * 1024
SUMS_LIMIT = 24 * 1024 * 1024
LINES_AT_ONCE = 8


def cas_table(count):
    steps = np.arange(count)
    angle = 2.0 * np.pi * (steps[:, None] * steps[None, :] % count) / count
    return (np.cos(angle) + np.sin(angle)).astype(np.float32)


def symbol(count):
    return (2.0 - 2.0 * np.cos(2.0 * np.pi * np.arange(count) / count)).astype(np.float32)


def block_base(height, chips, share, place):
    distance, flip = place
    core = lax.rem(height, 2)
    chip = lax.rem(height // 2 + distance * (1 - 2 * core) + chips, chips)
    return (chip * 2 + (1 - core if flip else core)) * share


def masked_line(orb_ref, line, live):
    parts = []
    for a in range(4):
        rows = orb_ref[line, a * 64 : (a + 1) * 64, :]
        parts.append(rows if a == 0 else jnp.where(a < live, rows, jnp.zeros((), BF16)))
    return jnp.concatenate(parts, axis=0)


def stage_kernel(live_ref, orb_hbm, orb_ref, order_ref, count_ref, sem):
    copy = pltpu.make_async_copy(orb_hbm, orb_ref, sem)
    copy.start()
    lines = orb_ref.shape[0]
    for n in range(4):
        count_ref[n] = 0

    def place(line, carry):
        n = live_ref[line] - 1
        order_ref[n, count_ref[n]] = line
        count_ref[n] += 1
        return carry

    lax.fori_loop(0, lines, place, 0)
    for n in range(4):
        for i in range(LINES_AT_ONCE):
            order_ref[n, count_ref[n] + i] = lines
    copy.wait()


def density_kernel(index_ref, live_ref, part_ref, orb_ref, *refs, chunk, places, chips):
    pieces, (cas_ref, dens_ref, spec_ref, table_ref) = refs[:-4], refs[-4:]
    packed_rows = table_ref.shape[0] // 2

    at = 0
    for piece in pieces:
        for first in range(0, piece.shape[0], 8):
            base = block_base(part_ref[2], chips, 8, places[at])
            at += 1
            both = piece[first : first + 8]
            table_ref[pl.ds(base, 8)] = both
            table_ref[pl.ds(packed_rows + base, 8)] = pltpu.roll(both, 64, 2)
    left_lanes = lax.broadcasted_iota(jnp.int32, (64, LANES), 1) < 64

    def body(i, carry):
        first = i * chunk
        rows_out = []
        for l in range(chunk):
            line = first + l
            phi = masked_line(orb_ref, line, live_ref[line])
            strips = []
            for a in range(4):
                halves = []
                for b in (0, 2):
                    at = line * 16 + a * 4 + b
                    halves.append(jnp.where(left_lanes, table_ref[index_ref[at]], table_ref[index_ref[at + 1]]))
                strips.append(jnp.concatenate(halves, axis=1))
            matrix = jnp.concatenate(strips, axis=0)
            product = jnp.dot(matrix, phi, preferred_element_type=F32)
            rows_out.append(jnp.sum(phi.astype(F32) * product, axis=0, keepdims=True))
        dens_ref[pl.ds(pl.multiple_of(first, 8), chunk), :] = jnp.concatenate(rows_out, axis=0)
        return carry

    lax.fori_loop(0, orb_ref.shape[0] // chunk, body, 0)
    spectrum = jnp.dot(dens_ref[...], cas_ref[...], precision=HIGHEST, preferred_element_type=F32)
    lines = spectrum.shape[0]
    wide = jnp.concatenate([spectrum, jnp.zeros((LANES - lines, spectrum.shape[1]), F32)], axis=0)
    spec_ref[...] = wide.T


def solve_kernel(part_ref, in_ref, cx_ref, cxt_ref, cz_ref, sx_ref, sz_ref, sy_ref, out_ref, *, cells_x, cells_z, cols, heights):
    core = part_ref[0]
    plane = part_ref[1]
    lane = lax.broadcasted_iota(jnp.int32, (cols, LANES), 1)
    group_of = lane // cells_z
    slots = LANES // cells_z
    skewed = [
        pltpu.roll(in_ref[pl.ds(h, cols, stride=heights), :], cells_z * h, 1) if h else in_ref[pl.ds(h, cols, stride=heights), :]
        for h in range(heights)
    ]
    rows = []
    for x in range(cells_x):
        mixed = jnp.zeros((cols, LANES), F32)
        for g in range(slots):
            mixed = jnp.where(group_of == g, skewed[(g - x) % slots], mixed)
        rows.append(pltpu.roll(mixed, LANES - cells_z * x, 1) if x else mixed)
    field = jnp.concatenate(rows, axis=0)
    forward = cx_ref[core]
    spec = jnp.dot(forward, field, precision=HIGHEST, preferred_element_type=F32)
    spec = jnp.dot(spec, cz_ref[...], precision=HIGHEST, preferred_element_type=F32)
    scale = sx_ref[core] + sz_ref[...] + sy_ref[plane]
    spec = spec / scale
    spec = jnp.dot(spec, cz_ref[...], precision=HIGHEST, preferred_element_type=F32)
    back = jnp.dot(cxt_ref[core], spec, precision=HIGHEST, preferred_element_type=F32)
    skewed = []
    for x in range(cells_x):
        part = back[x * cols : (x + 1) * cols]
        skewed.append(pltpu.roll(part, cells_z * x, 1) if x else part)
    for h in range(heights):
        mixed = jnp.zeros((cols, LANES), F32)
        for x in range(cells_x):
            mixed = jnp.where(group_of == (h + x) % slots, skewed[x], mixed)
        mixed = pltpu.roll(mixed, LANES - cells_z * h, 1) if h else mixed
        out_ref[pl.ds(h, cols, stride=heights), :] = mixed


def hamiltonian_kernel(
    pair_ref,
    order_ref,
    count_ref,
    part_ref,
    orb_ref,
    dens_ref,
    back_ref,
    cas_ref,
    pot_ref,
    keep_ref,
    first_ref,
    rest_ref,
    left_ref,
    right_ref,
    padded_ref,
    *,
    places,
    chips,
):
    lines = dens_ref.shape[0]

    def clear(i, carry):
        left_ref[pl.ds(i * 8, 8)] = jnp.zeros((8, 64, LANES), F32)
        right_ref[pl.ds(i * 8, 8)] = jnp.zeros((8, 64, LANES), F32)
        return carry

    lax.fori_loop(0, left_ref.shape[0] // 8, clear, 0)
    hartree = jnp.dot(cas_ref[...], back_ref[...], precision=HIGHEST, preferred_element_type=F32).T
    dens = dens_ref[...]
    potential = hartree[:lines] - XC_COEF * jnp.exp(jnp.log(dens * dens + 1.0) * (1.0 / 6.0))
    pot_ref[...] = potential
    padded_ref[...] = jnp.concatenate([potential, jnp.zeros((padded_ref.shape[0] - lines, LANES), F32)], axis=0)

    for n in range(1, 5):

        def body(i, carry, n=n):
            for j in range(LINES_AT_ONCE):
                entry = order_ref[n - 1, i * LINES_AT_ONCE + j]
                line = jnp.minimum(entry, lines - 1)
                rows = orb_ref[line, : n * 64, :]
                phi = rows if n % 2 == 0 else jnp.concatenate([rows, jnp.zeros((64, LANES), BF16)], axis=0)
                weighted = (rows.astype(F32) * padded_ref[pl.ds(entry, 1), :]).astype(BF16)
                full = lax.dot_general(weighted, phi, (((1,), (1,)), ((), ())), preferred_element_type=F32)
                for a in range(n):
                    for b in range(0, n, 2):
                        at = line * 16 + a * 4 + b
                        both = full[a * 64 : (a + 1) * 64, b * 64 : b * 64 + LANES]
                        left_ref[pair_ref[at]] += both
                        if b + 1 < n:
                            right_ref[pair_ref[at + 1]] += both
            return carry

        lax.fori_loop(0, (count_ref[n - 1] + LINES_AT_ONCE - 1) // LINES_AT_ONCE, body, 0)
    left_lanes = lax.broadcasted_iota(jnp.int32, (8, 64, LANES), 2) < 64

    def emit(base):
        low, high = pl.ds(base, 8), pl.ds(base + 8, 8)
        crossed = jnp.where(left_lanes, left_ref[high], right_ref[low])
        return jnp.where(left_lanes, left_ref[low], right_ref[high]) + pltpu.roll(crossed, 64, 2)

    at = 0
    for out in (keep_ref, first_ref, rest_ref):
        for first in range(0, out.shape[0], 8):
            out[first : first + 8] = emit(block_base(part_ref[2], chips, 16, places[at])).astype(out.dtype)
            at += 1


def finish_kernel(keep_ref, got_ref, one_ref, two_ref, twin_one_ref, twin_two_ref, out_ref):
    rows = out_ref.shape[0] // 2
    for i in range(rows):
        total = keep_ref[keep_ref.shape[0] - rows + i] + got_ref[got_ref.shape[0] - rows + i].astype(F32)
        total = total + one_ref[rows + i].astype(F32) + two_ref[i].astype(F32)
        total = total + twin_one_ref[i].astype(F32) + twin_two_ref[i].astype(F32)
        out_ref[i] = total[:, :64]
        out_ref[rows + i] = total[:, 64:]


def per_device(orbitals, live_atoms, pair_index, density_blocks):
    cells_x, cells_z, width, line_cells = orbitals.shape
    cols = lax.axis_size("col")
    heights = lax.axis_size("height")
    full_x = cells_x * cols
    full_z = cells_z * heights
    lines = cells_x * cells_z
    share = density_blocks.shape[0]
    devices = cols * heights
    copies = devices // line_cells
    chunk = 16
    block_rows = share * heights // 2

    cas_y = cas_table(line_cells)
    cas_y2 = np.repeat(cas_y, copies, axis=1)
    cas_x = cas_table(full_x)
    order = np.arange(full_x).reshape(cols, cells_x).T.reshape(-1)
    half_x = full_x // copies
    forward_x = cas_x.reshape(copies, half_x, full_x)[:, :, order]
    back_x = forward_x.transpose(0, 2, 1).copy()
    cas_z = cas_table(full_z)
    norm = 1.0 / (full_x * full_z * line_cells)
    unit = FOUR_PI * norm
    sym_x = np.broadcast_to(symbol(full_x).reshape(copies, half_x, 1) / unit, (copies, half_x, LANES)).astype(np.float32)
    sym_z = ((symbol(full_z) + KAPPA * KAPPA) / unit).reshape(1, full_z).astype(np.float32)
    sym_y = (symbol(line_cells) / unit).astype(np.float32)

    orb = orbitals.reshape(lines, width, line_cells)
    live = live_atoms.reshape(lines)
    pairs = pair_index.reshape(lines * 16)
    packed = jnp.concatenate([density_blocks[: share // 2], density_blocks[share // 2 :]], axis=2)
    chips = heights // 2
    far = chips // 2
    height = lax.axis_index("height")
    device = lax.axis_index("col") * heights + height
    part = jnp.stack([device % copies, device // copies, height]).astype(jnp.int32)
    twin = [(h, h ^ 1) for h in range(heights)]

    def across(values):
        return lax.ppermute(values, "height", twin)

    def onward(values, hops, sign=1, flip=0):
        def target(h):
            core = h % 2
            return (h // 2 + sign * hops * (1 - 2 * core)) % chips * 2 + (core ^ flip)

        return lax.ppermute(values, "height", [(h, target(h)) for h in range(heights)])

    half = share // 2
    gather_places = [(0, 0), (0, 1)]
    gather_places += [(-2, 0), (2, 1), (-2, 1), (2, 0), (-1, 0), (-1, 1), (1, 1), (1, 0)]
    gather_places += [(-3, 0), (3, 1), (-3, 1), (3, 0)]
    gather_places += [(far, 0), (far, 1)]
    keep_places = [(far, 0), (3, 0), (1, 0), (3, 1), (1, 1), (2, 0), (2, 1), (0, 0)]
    sum_places = keep_places + [(-d, 1 - flip) for d, flip in keep_places]

    side = jnp.arange(lines * 16, dtype=jnp.int32) % 2
    table_index = (pairs // share) * half + pairs % half
    table_index = table_index + jnp.where((pairs // half) % 2 == side, 0, block_rows)
    twin_packed = across(packed)
    second = onward(packed, 2)
    second_twin = onward(twin_packed, 2)
    whole_chip = jnp.concatenate([packed, twin_packed], axis=0)
    near = onward(whole_chip, 1)
    smem = pl.BlockSpec(memory_space=pltpu.SMEM)
    vmem = pl.BlockSpec(memory_space=pltpu.VMEM)
    params = pltpu.CompilerParams(vmem_limit_bytes=VMEM_LIMIT)
    orb, order, count = pl.pallas_call(
        stage_kernel,
        in_specs=[smem, pl.BlockSpec(memory_space=pl.ANY)],
        out_specs=[vmem, smem, smem],
        out_shape=[
            jax.ShapeDtypeStruct(orb.shape, BF16),
            jax.ShapeDtypeStruct((4, lines + LINES_AT_ONCE), jnp.int32),
            jax.ShapeDtypeStruct((4,), jnp.int32),
        ],
        scratch_shapes=[pltpu.SemaphoreType.DMA(())],
        compiler_params=pltpu.CompilerParams(vmem_limit_bytes=STAGE_LIMIT),
        name="stage",
    )(live, orb)
    second_twin, near, table_index, live, part, pairs, orb, order, count = lax.optimization_barrier(
        (second_twin, near, table_index, live, part, pairs, orb, order, count)
    )
    fourth = onward(second, 2)
    rest = [onward(second, 1), onward(second_twin, 1)]
    pieces = [whole_chip]
    for piece in (second, second_twin, near, *rest, fourth):
        pieces += [piece, across(piece)]
    density, spectrum = pl.pallas_call(
        functools.partial(density_kernel, chunk=chunk, places=gather_places, chips=chips),
        in_specs=[smem] * 3 + [vmem] * (len(pieces) + 2),
        out_specs=[vmem, vmem],
        out_shape=[
            jax.ShapeDtypeStruct((lines, line_cells), F32),
            jax.ShapeDtypeStruct((devices, LANES), F32),
        ],
        scratch_shapes=[pltpu.VMEM((2 * block_rows, 64, LANES), BF16)],
        compiler_params=params,
        name="density",
    )(table_index, live, part, orb, *pieces, jnp.asarray(cas_y2))

    def exchange(values):
        out = lax.all_to_all(values.reshape(devices, 1, LANES), ("col", "height"), split_axis=0, concat_axis=0, tiled=True)
        return out.reshape(devices, LANES)

    solved = pl.pallas_call(
        lambda *refs: solve_kernel(*refs, cells_x=cells_x, cells_z=cells_z, cols=cols, heights=heights),
        in_specs=[smem, vmem, vmem, vmem, vmem, vmem, vmem, smem],
        out_specs=vmem,
        out_shape=jax.ShapeDtypeStruct((devices, LANES), F32),
        compiler_params=params,
        name="solve",
    )(
        part,
        exchange(spectrum),
        jnp.asarray(forward_x),
        jnp.asarray(back_x),
        jnp.asarray(cas_z),
        jnp.asarray(sym_x),
        jnp.asarray(sym_z),
        jnp.asarray(sym_y),
    )
    returned = exchange(solved)

    half_rows = block_rows // 2
    potential, keep, give_first, give_rest = pl.pallas_call(
        functools.partial(hamiltonian_kernel, places=sum_places, chips=chips),
        in_specs=[smem] * 4 + [vmem] * 4,
        out_specs=[vmem] * 4,
        out_shape=[
            jax.ShapeDtypeStruct((lines, line_cells), F32),
            jax.ShapeDtypeStruct((half_rows, 64, LANES), F32),
            jax.ShapeDtypeStruct((2 * share, 64, LANES), BF16),
            jax.ShapeDtypeStruct((half_rows - 2 * share, 64, LANES), BF16),
        ],
        scratch_shapes=[
            pltpu.VMEM((2 * block_rows, 64, LANES), F32),
            pltpu.VMEM((2 * block_rows, 64, LANES), F32),
            pltpu.VMEM((lines + 8, LANES), F32),
        ],
        compiler_params=pltpu.CompilerParams(vmem_limit_bytes=SUMS_LIMIT),
        name="hamiltonian",
    )(pairs, order, count, part, orb, density, returned, jnp.asarray(cas_y2))

    got_first = across(give_first)
    got_rest = across(lax.optimization_barrier((give_rest, got_first))[0])

    def local(kept, i, count=1):
        got = got_first[i * half : (i + count) * half] if i < 4 else got_rest[(i - 4) * half : (i - 4 + count) * half]
        return kept[i * half : (i + count) * half] + got.astype(F32)

    begin = lax.optimization_barrier((keep, local(keep, 0).astype(BF16), local(keep, 1, 3).astype(BF16)))
    far_sum = onward(begin[1], 2)
    ahead = onward(begin[2], 1)
    third_twin = ahead[2 * half :]
    ones = lax.optimization_barrier((begin[0], local(begin[0], 4).astype(BF16)))
    by_one_twin = onward(ones[1], 1, 1, 1)
    twos = lax.optimization_barrier((ones[0], (local(ones[0], 6) + third_twin.astype(F32)).astype(BF16)))
    by_two_twin = onward(twos[1], 2, 1, 1)
    by_two = onward((local(twos[0], 5) + far_sum.astype(F32) + ahead[:half].astype(F32)).astype(BF16), 2)
    hamiltonian = pl.pallas_call(
        finish_kernel,
        in_specs=[vmem] * 6,
        out_specs=vmem,
        out_shape=jax.ShapeDtypeStruct(density_blocks.shape, F32),
        compiler_params=params,
        name="finish",
    )(keep, got_rest, ahead, by_two, by_one_twin, by_two_twin)
    return potential.reshape(cells_x, cells_z, line_cells), hamiltonian


def solution(mesh):
    placed = (
        P("col", "height", None, None),
        P("col", "height"),
        P("col", "height", None, None),
        P(("col", "height"), None, None),
    )
    return jax.shard_map(
        per_device,
        mesh=mesh,
        in_specs=placed,
        out_specs=(P("col", "height", None), P(("col", "height"), None, None)),
        check_vma=False,
    )
```
